256 devices in a mesh: section: 4 (over z_lo, core), replica: 64 (over z_hi, y, x).
Axes of the slice: x: 4, y: 4, z: 8 (z_hi: 4, z_lo: 2; z = z_hi * 2 + z_lo), core: 2. Of those that a mesh axis runs over, the one named last changes fastest.
Arguments:
- embeddings: bfloat16 [64, 4, 32, 2048], P('replica'), may hold values from -6 to 6
- cotangent: bfloat16 [64, 4, 32, 2048], P('replica'), may hold values from -6 to 6
- plan: int32 [64, 4], P('replica'), may hold values from 0 to 3, each once within a row
- doc_ids: int32 [64, 4, 32], P('replica'), may hold values from 0 to 3, never falling along the last dimension, each value on 1 to 16 neighbouring positions
- norm_gain: bfloat16 [4, 2048], P('section'), may hold values from 0.099609375 to 1.8984375
- w_query: bfloat16 [4, 2048, 1024], P('section', 'replica'), may hold values from -0.125 to 0.125
- w_out: bfloat16 [4, 1024, 2048], P('section', 'replica'), may hold values from -0.1875 to 0.1875
- kv_stash: bfloat16 [4, 2048, 512], P('section'), may hold values from -0.125 to 0.125
- kv_now: bfloat16 [4, 2048, 512], P('section'), may hold values from -0.125 to 0.125
- adam_m: bfloat16 [4, 2048, 512], P('section', 'replica'), may hold values from -3 to 3
- adam_v: bfloat16 [4, 2048, 512], P('section', 'replica'), may hold values from 0.25 to 4
Outputs:
- stash_next: bfloat16 [4, 2048, 512], P('section')
- current_next: bfloat16 [4, 2048, 512], P('section')
- moment_first: bfloat16 [4, 2048, 512], P('section', 'replica')
- moment_second: bfloat16 [4, 2048, 512], P('section', 'replica')
The draws below stay inside these ranges and needn't reach their ends.
Inputs may be any that keep to these rules, and one draw needn't show every extreme that they name: `plan`: each row orders the 4 sequences of a replica, each once. `doc_ids`: never falling along a sequence; each document has 1 to 16 tokens.
All inputs are finite; a program needn't handle non-finite values.
Results may differ from the reference program's by a relative error of at most 0.024.
Values may be sent and summed in bfloat16 or wider, within the bound.
A program may use at most 128 MiB of HBM per device.

```python
import math
import jax
import jax.numpy as jnp
import numpy as np
from jax import lax

D = 2048
HEAD = 64
SEQ = 32
MICRO = 2
DOCS = 4
QW = 1024
KVW2 = 512
SLOTS = 4
SECTIONS = 4
REPLICAS = 64


def steps_of(rng, dims, pieces, low, high):
    def one(position, parts):
        steps = jax.random.uniform(jax.random.fold_in(jax.random.fold_in(rng, 6), position), (parts,), jnp.float32, low / len(pieces), high / len(pieces))
        return jnp.repeat(jnp.exp(steps), dims[position] // parts).reshape((-1,) + (1,) * (len(dims) - position - 1))

    level = one(*pieces[0])
    for cut in pieces[1:]:
        level = level * one(*cut)
    return level


def profile(number_of, total, most, slope):
    loads = [(1 << 20) // math.isqrt(standing ** slope) + 1 for standing in range(2, number_of + 1)]
    rest, given = total - most - (number_of - 1), [1] * (number_of - 1)
    while rest > 0:
        candidates = [i for i in range(number_of - 1) if given[i] < most]
        mass, budget = sum([loads[i] for i in candidates]), rest
        for i in candidates:
            extra = min(most - given[i], max(1, budget * loads[i] // mass), rest)
            given[i] = given[i] + extra
            rest = rest - extra
    return np.array([most] + given)


def uneven_parts(key, count, total, reach, lean):
    if count == 2:
        one = jax.random.randint(key, (), max(1, total - reach), min(reach, total - 1) + 1)
        return jnp.stack([one, total - one])
    sizes = jnp.asarray(profile(count, total, reach, lean), jnp.int32)
    pairs = (count - 1) // 2
    donor, sink = sizes[1:1 + 2 * pairs:2], sizes[2:2 + 2 * pairs:2]
    room = jnp.minimum(donor - 1, reach - sink)
    passed = jax.random.randint(jax.random.fold_in(key, 1), (pairs,), 0, 1 << 20) % (room + 1)
    sizes = sizes.at[1:1 + 2 * pairs:2].set(donor - passed).at[2:2 + 2 * pairs:2].set(sink + passed)
    return sizes[jax.random.permutation(jax.random.fold_in(key, 2), count)]


def noise(own_key, shape, scale, limit, cuts=(), held_as=jnp.bfloat16):
    values = scale * jax.random.normal(own_key, shape, jnp.float32)
    if cuts:
        values = values * steps_of(own_key, shape, cuts, -0.22, 0.18)
    return jnp.clip(values, -limit, limit).astype(held_as)


def setup_inputs(seed: int = 0) -> dict:
    key_of = jax.random.split(jax.random.key(seed), 12)
    return {
        "embeddings": noise(key_of[0], (REPLICAS, SLOTS, SEQ, D), 1.0, 6.0, ((0, 64),)),
        "cotangent": noise(key_of[1], (REPLICAS, SLOTS, SEQ, D), 1.0, 6.0, ((0, 64),)),
        "plan": jax.vmap(lambda own: jax.random.permutation(own, SLOTS))(jax.random.split(key_of[2], REPLICAS)).reshape((REPLICAS, SLOTS)).astype(jnp.int32),
        "doc_ids": jax.vmap(lambda own: jnp.searchsorted(jnp.cumsum(uneven_parts(own, DOCS, SEQ, SEQ // 2, 0)), jnp.arange(SEQ), side="right"))(jax.random.split(key_of[3], REPLICAS * SLOTS)).reshape((REPLICAS, SLOTS, SEQ)).astype(jnp.int32),
        "norm_gain": jnp.clip(1.0 + 0.18 * jax.random.normal(key_of[4], (SECTIONS, D), jnp.float32), 0.099609375, 1.8984375).astype(jnp.bfloat16),
        "w_query": noise(key_of[5], (SECTIONS, D, QW), D ** -0.5, 0.125, ((0, 4), (1, 64))),
        "w_out": noise(key_of[6], (SECTIONS, QW, D), QW ** -0.5, 0.1875, ((0, 4), (1, 64))),
        "kv_stash": noise(key_of[7], (SECTIONS, D, KVW2), D ** -0.5, 0.125, ((0, 4),)),
        "kv_now": noise(key_of[8], (SECTIONS, D, KVW2), D ** -0.5, 0.125, ((0, 4),)),
        "adam_m": noise(key_of[9], (SECTIONS, D, KVW2), 0.5, 3.0, ((0, 4), (1, 64))),
        "adam_v": jnp.clip(jnp.exp(math.log(4.0) - 2.7725887 * jax.random.uniform(key_of[10], (SECTIONS, D, KVW2), jnp.float32) ** steps_of(key_of[10], (SECTIONS, D, KVW2), ((0, 4), (1, 64)), -0.2, 0.2)), 0.25, 4.0).astype(jnp.bfloat16),
    }


beta_first = 0.9
beta_second = 0.999
learn_rate = 0.003
adam_eps = 1e-08
norm_eps = 1e-05

def pre_norm(wide_hidden, gain):
    return wide_hidden * lax.rsqrt(lax.optimization_barrier(jnp.mean(wide_hidden * wide_hidden, axis=-1, keepdims=True)) + norm_eps) * gain.astype(jnp.float32)

def attend_core(query_wide, paired_wide, doc_row):
    length = query_wide.shape[0]
    queries = query_wide.astype(jnp.bfloat16)
    paired = paired_wide.astype(jnp.bfloat16)
    kv_heads = paired.shape[1] // (2 * HEAD)
    query_heads = queries.reshape(length, kv_heads, -1, HEAD).astype(jnp.float32)
    keys = paired[:, :kv_heads * HEAD].reshape(length, kv_heads, HEAD).astype(jnp.float32)
    values = paired[:, kv_heads * HEAD:].reshape(length, kv_heads, HEAD).astype(jnp.float32)
    scores = jnp.einsum('tgsd,ugd->gstu', query_heads, keys) * HEAD ** (-0.5)
    places = jnp.arange(length)
    allowed = (places[:, None] >= places[None, :]) & (doc_row[:, None] == doc_row[None, :])
    weight = jnp.where(allowed, jnp.exp(scores), 0.0)
    probs = (weight / lax.optimization_barrier(jnp.sum(weight, axis=-1, keepdims=True))).astype(jnp.bfloat16)
    mixed = jnp.einsum('gstu,ugd->tgsd', probs.astype(jnp.float32), values)
    return mixed.reshape(length, -1)

def project_in(hidden, weights, query_weight, gain):
    wide_hidden = hidden.astype(jnp.float32)
    normed = pre_norm(wide_hidden, gain).astype(jnp.bfloat16)
    paired = jnp.dot(normed, weights, preferred_element_type=jnp.float32).astype(jnp.bfloat16)
    queries = jnp.dot(normed, query_weight, preferred_element_type=jnp.float32).astype(jnp.bfloat16)
    return (wide_hidden, normed, paired, queries)

def forward(hidden, weights, query_weight, output_weight, gain, doc_row):
    wide_hidden, normed, paired, queries = project_in(hidden, weights, query_weight, gain)
    mixed = attend_core(queries.astype(jnp.float32), paired.astype(jnp.float32), doc_row).astype(jnp.bfloat16)
    result = wide_hidden + jnp.dot(mixed, output_weight, preferred_element_type=jnp.float32)
    return result.astype(jnp.bfloat16)

def backward(hidden, upstream, weights, query_weight, output_weight, gain, doc_row):
    wide_hidden, normed, paired, queries = project_in(hidden, weights, query_weight, gain)
    mixed_grad = lax.dot_general(upstream, output_weight, (((1,), (1,)), ((), ())), preferred_element_type=jnp.float32)

    def local_core(query_in, paired_in):
        return attend_core(query_in, paired_in, doc_row)
    unused, pull_back = jax.vjp(local_core, queries.astype(jnp.float32), paired.astype(jnp.float32))
    grad_query, grad_paired = pull_back(mixed_grad)
    key_grad = grad_paired.astype(jnp.bfloat16)
    query_grad = grad_query.astype(jnp.bfloat16)
    grad_normed = lax.dot_general(query_grad, query_weight, (((1,), (1,)), ((), ())), preferred_element_type=jnp.float32)
    grad_normed = grad_normed + lax.dot_general(key_grad, weights, (((1,), (1,)), ((), ())), preferred_element_type=jnp.float32)

    def local_norm(hidden_in):
        return pre_norm(hidden_in, gain)
    unused_norm, norm_back = jax.vjp(local_norm, wide_hidden)
    grad_through, = norm_back(grad_normed)
    return ((upstream.astype(jnp.float32) + grad_through).astype(jnp.bfloat16), normed, key_grad)

def step_gradient(weights_all, embeddings, cotangent, plan, doc_ids, norm_gain, w_query, w_out, which_step):

    def one_replica(carry, inputs):
        embed_rows, cot_rows, order, doc_rows = inputs
        normed_parts = [[] for section_index in range(SECTIONS)]
        key_parts = [[] for section_index in range(SECTIONS)]
        for micro_index in range(MICRO):
            chosen = order[which_step * MICRO + micro_index]
            hidden = embed_rows[chosen]
            doc_row = doc_rows[chosen]
            inputs_kept = []
            for section_index in range(SECTIONS):
                inputs_kept.append(hidden)
                if section_index < SECTIONS - 1:
                    hidden = forward(hidden, weights_all[section_index], w_query[section_index], w_out[section_index], norm_gain[section_index], doc_row)
            upstream = cot_rows[chosen]
            for section_index in reversed(range(SECTIONS)):
                upstream, normed, key_grad = backward(inputs_kept[section_index], upstream, weights_all[section_index], w_query[section_index], w_out[section_index], norm_gain[section_index], doc_row)
                normed_parts[section_index].append(normed)
                key_parts[section_index].append(key_grad)
        summed = []
        for section_index in range(SECTIONS):
            normed_all = jnp.concatenate(normed_parts[section_index], axis=0)
            key_all = jnp.concatenate(key_parts[section_index], axis=0)
            summed.append(lax.dot_general(normed_all, key_all, (((0,), (0,)), ((), ())), preferred_element_type=jnp.float32))
        return (carry + jnp.stack(summed), None)
    start_sum = jnp.zeros(weights_all.shape, jnp.float32)
    total, unused = lax.scan(one_replica, start_sum, (embeddings, cotangent, plan, doc_ids))
    return total / REPLICAS

def adam_update(weights, first, second, gradient):
    first_new = beta_first * first.astype(jnp.float32) + (1.0 - beta_first) * gradient
    second_new = beta_second * second.astype(jnp.float32) + (1.0 - beta_second) * gradient * gradient
    moved = weights.astype(jnp.float32) - learn_rate * first_new / (jnp.sqrt(second_new) + adam_eps)
    return (moved.astype(jnp.bfloat16), first_new.astype(jnp.bfloat16), second_new.astype(jnp.bfloat16))

def reference(embeddings, cotangent, plan, doc_ids, norm_gain, w_query, w_out, kv_stash, kv_now, adam_m, adam_v):
    grad_zero = step_gradient(kv_stash, embeddings, cotangent, plan, doc_ids, norm_gain, w_query, w_out, 0)
    grad_one = step_gradient(kv_now, embeddings, cotangent, plan, doc_ids, norm_gain, w_query, w_out, 1)
    stash_next, first_mid, second_mid = adam_update(kv_now, adam_m, adam_v, grad_zero)
    current_next, moment_first, moment_second = adam_update(stash_next, first_mid, second_mid, grad_one)
    return (stash_next, current_next, moment_first, moment_second)
```

```python
import functools

import jax
import jax.numpy as jnp
from jax import lax
from jax.experimental import pallas as pl
from jax.experimental.pallas import tpu as pltpu
from jax.sharding import PartitionSpec as P

HEAD = 64
RING = 4
REPLICAS = 64
TOKENS = 128
HALF = 64
WIDTH = 2048
QW = 1024
KVW = 512
TILE = 256
BF = jnp.bfloat16
F32 = jnp.float32
MESH = pl.DeviceIdType.MESH

beta_first = 0.9
beta_second = 0.999
learn_rate = 0.003
adam_eps = 1e-08
norm_eps = 1e-05

NN = (((1,), (0,)), ((), ()))
NT = (((1,), (1,)), ((), ()))
TN = (((0,), (0,)), ((), ()))


def mm(a, b, dims=NN):
    return lax.dot_general(a, b, dims, preferred_element_type=F32)


def wrap(v):
    return lax.rem(v + RING, RING)


class Place:
    def __init__(self):
        me = lax.axis_index("replica")
        self.z = me // 16
        self.y = lax.rem(me // 4, RING)
        self.x = lax.rem(me, RING)
        self.me = me

    def at(self, **moves):
        z = wrap(self.z + moves["z"]) if "z" in moves else self.z
        y = wrap(self.y + moves["y"]) if "y" in moves else self.y
        x = wrap(self.x + moves["x"]) if "x" in moves else self.x
        return (z * RING + y) * RING + x


class Gather:
    def __init__(self, place, parts, send, recv):
        self.place, self.parts, self.send, self.recv = place, parts, send, recv

    def chunk(self, k, src):
        ref, rows, order = self.parts[k]
        return ref.at[pl.ds(pl.multiple_of(src * rows, rows), rows), :]

    def copy(self, k, src, dst):
        piece = self.chunk(k, src)
        return pltpu.make_async_remote_copy(
            src_ref=piece,
            dst_ref=piece,
            send_sem=self.send.at[k],
            recv_sem=self.recv.at[k, src],
            device_id={"replica": dst},
            device_id_type=MESH,
        )

    def push(self, k, src, *axes):
        for axis in axes:
            for step in (1, -1):
                self.copy(k, src, self.place.at(**{axis: step})).start()

    def arrived(self, k, src):
        self.copy(k, src, self.place.at(x=1)).wait_recv()

    def begin(self):
        for k in range(len(self.parts)):
            u, v = self.parts[k][2]
            self.push(k, self.place.me, "z", u, v)

    def finish(self):
        at = self.place.at
        count = len(self.parts)
        for k in range(count):
            u, v = self.parts[k][2]
            for step in (-1, 1):
                self.arrived(k, at(z=step))
                self.push(k, at(z=step), u, v)
            off = 2 * (k % 2) - 1
            self.copy(k, at(z=off), at(z=-off)).start()
        for k in range(count):
            u, v = self.parts[k][2]
            self.arrived(k, at(z=2))
            self.push(k, at(z=2), u, v)

        def near_u(dz, carry):
            for k in range(count):
                u, v = self.parts[k][2]
                for step in (-1, 1):
                    self.arrived(k, at(**{"z": dz, u: step}))
                    self.push(k, at(**{"z": dz, u: step}), v)
                off = 2 * lax.rem(self.place.z + dz, 2) - 1
                self.copy(k, at(**{"z": dz, u: off}), at(**{u: -off})).start()
            return carry

        def far_u(dz, carry):
            for k in range(count):
                u, v = self.parts[k][2]
                self.arrived(k, at(**{"z": dz, u: 2}))
                self.push(k, at(**{"z": dz, u: 2}), v)
            return carry

        def near_v(i, carry):
            dz, du = i // RING, lax.rem(i, RING)
            for k in range(count):
                u, v = self.parts[k][2]
                for step in (-1, 1):
                    self.arrived(k, at(**{"z": dz, u: du, v: step}))
                pos_u = self.place.x if u == "x" else self.place.y
                off = 2 * lax.rem(self.place.z + dz + pos_u + du, 2) - 1
                self.copy(k, at(**{"z": dz, u: du, v: off}), at(**{v: -off})).start()
            return carry

        def far_v(i, carry):
            dz, du = i // RING, lax.rem(i, RING)
            for k in range(count):
                u, v = self.parts[k][2]
                self.arrived(k, at(**{"z": dz, u: du, v: 2}))
            return carry

        lax.fori_loop(0, RING, near_u, 0)
        lax.fori_loop(0, RING, far_u, 0)
        lax.fori_loop(0, RING * RING, near_v, 0)
        lax.fori_loop(0, RING * RING, far_v, 0)

    def drain(self):
        for k in range(len(self.parts)):
            ref, rows, order = self.parts[k]
            sent = ref.at[pl.ds(0, (REPLICAS - 1) * rows), :]
            pltpu.make_async_remote_copy(
                src_ref=sent,
                dst_ref=sent,
                send_sem=self.send.at[k],
                recv_sem=self.recv.at[k, 0],
                device_id={"replica": self.place.at(x=1)},
                device_id_type=MESH,
            ).wait_send()


class Exchange:
    def __init__(self, place, axis, out, into, send, recv):
        self.place, self.axis, self.out, self.into = place, axis, out, into
        self.send, self.recv = send, recv
        self.mine = {"x": place.x, "y": place.y, "z": place.z}[axis]

    def copies(self):
        for step in (1, 3, 2):
            there = wrap(self.mine + step)
            source = self.out(there)
            yield there, step, pltpu.make_async_remote_copy(
                src_ref=source,
                dst_ref=self.into.at[self.mine],
                send_sem=self.send.at[step - 1],
                recv_sem=self.recv.at[step - 1],
                device_id={"replica": self.place.at(**{self.axis: step})},
                device_id_type=MESH,
            )

    def start(self):
        for there, step, copy in self.copies():
            copy.start()

    def wait(self):
        for there, step, copy in self.copies():
            copy.wait_recv()
        for there, step, copy in self.copies():
            copy.wait_send()


def lower_lanes(shape):
    return lax.broadcasted_iota(jnp.int32, shape, len(shape) - 1) < HEAD


def both_halves(block, half):
    low = lower_lanes(block.shape)
    wide = block.astype(F32)
    own = jnp.where(low, wide, 0.0) if half == 0 else jnp.where(low, 0.0, wide)
    return (own + pltpu.roll(own, HEAD, 1)).astype(BF)


def head_rows(ref, group):
    blocks = []
    for j in range(4):
        start = (2 * group + j // 2) * 128
        block = ref[:, start : start + 128]
        low = lower_lanes(block.shape)
        zero = jnp.zeros_like(block)
        blocks.append(jnp.where(low, block, zero) if j % 2 == 0 else jnp.where(low, zero, block))
    return jnp.concatenate(blocks, axis=0)


def put_heads(ref, group, rows):
    low = lower_lanes((TOKENS, 128))
    for b in range(2):
        first = rows[2 * b * TOKENS : (2 * b + 1) * TOKENS]
        second = rows[(2 * b + 1) * TOKENS : (2 * b + 2) * TOKENS]
        start = (2 * group + b) * 128
        ref[:, start : start + 128] = jnp.where(low, first, second).astype(BF)


def kernel(
    emb,
    cot,
    plan,
    mask,
    gain,
    wq_share,
    wo_share,
    kv_stash,
    kv_now,
    adam_m,
    adam_v,
    stash_out,
    next_out,
    m_out,
    v_out,
    wq,
    wo,
    hid,
    up,
    fwd_out,
    bwd_out,
    normed,
    scale,
    q,
    kv,
    probs,
    mixed,
    mixed_grad,
    dq,
    dnormed,
    n_send_buf,
    n_all,
    k_all,
    x_buf,
    x_all,
    z_buf,
    z_all,
    w_send,
    w_recv,
    o_send,
    o_recv,
    hop_send,
    hop_recv,
    n_send,
    n_recv,
    k_send,
    k_recv,
    x_send,
    x_recv,
    z_send,
    z_recv,
):
    place = Place()
    section = lax.axis_index("section")
    last = RING - 1

    barrier = pltpu.get_barrier_semaphore()
    for axis in ("x", "y", "z"):
        for step in (1, 2, 3):
            pl.semaphore_signal(
                barrier, inc=1, device_id={"replica": place.at(**{axis: step})}, device_id_type=MESH
            )
    for step in (1, -1):
        pl.semaphore_signal(
            barrier, inc=1, device_id={"section": wrap(section + step)}, device_id_type=MESH
        )
    pl.semaphore_wait(barrier, 11)

    weights = Gather(place, [(wq, 32, ("x", "y")), (wo, 16, ("y", "x"))], w_send, w_recv)
    weights.chunk(0, place.me)[...] = wq_share[0]
    weights.chunk(1, place.me)[...] = wo_share[0]
    weights.begin()

    def norm_and_kv():
        def rows_of(i, carry):
            rows = pl.ds(i * 16, 16)
            wide = hid[rows, :].astype(F32)
            r = lax.rsqrt(jnp.mean(wide * wide, axis=-1, keepdims=True) + norm_eps)
            scale[rows, :] = jnp.broadcast_to(r, (16, 128))
            normed[rows, :] = (wide * r * gain[...].astype(F32)).astype(BF)
            return carry

        lax.fori_loop(0, TOKENS // 16, rows_of, 0)

        def tile(j, carry):
            cols = pl.ds(pl.multiple_of(j * TILE, TILE), TILE)
            kv[:HALF, cols] = mm(normed[:HALF, :], kv_stash[0, :, cols]).astype(BF)
            kv[HALF:, cols] = mm(normed[HALF:, :], kv_now[0, :, cols]).astype(BF)
            return carry

        lax.fori_loop(0, KVW // TILE, tile, 0)

    @pl.when(section == 0)
    def _():
        for i in range(RING):
            hid[i * 32 : (i + 1) * 32, :] = emb[0, plan[0, i]]
        norm_and_kv()

    @pl.when(section == last)
    def _():
        for i in range(RING):
            up[i * 32 : (i + 1) * 32, :] = cot[0, plan[0, i]]

    weights.finish()

    @pl.when(section > 0)
    def _():
        pltpu.make_async_remote_copy(
            src_ref=hid,
            dst_ref=hid,
            send_sem=hop_send.at[0],
            recv_sem=hop_recv.at[0],
            device_id={"section": wrap(section - 1)},
            device_id_type=MESH,
        ).wait_recv()
        norm_and_kv()

    def q_tile(j, carry):
        cols = pl.ds(pl.multiple_of(j * TILE, TILE), TILE)
        q[:, cols] = mm(normed[...], wq[:, cols]).astype(BF)
        return carry

    lax.fori_loop(0, QW // TILE, q_tile, 0)

    for group in range(4):
        start = (group // 2) * 128
        keys = both_halves(kv[:, start : start + 128], group % 2)
        values = both_halves(kv[:, 256 + start : 256 + start + 128], group % 2)
        score = mm(head_rows(q, group), keys, NT).reshape(4, TOKENS, TOKENS)
        weight = jnp.where(mask[...][None] > 0, jnp.exp(score * (HEAD**-0.5)), 0.0)
        prob = weight / jnp.sum(weight, axis=-1, keepdims=True)
        prob = prob.reshape(4 * TOKENS, TOKENS)
        probs[group] = prob

        @pl.when(section < last)
        def _():
            put_heads(mixed, group, mm(prob.astype(BF), values))

    @pl.when(section < last)
    def _():
        def out_tile(j, carry):
            cols = pl.ds(pl.multiple_of(j * TILE, TILE), TILE)
            total = hid[:, cols].astype(F32) + mm(mixed[...], wo[:, cols])
            fwd_out[:, cols] = total.astype(BF)
            pltpu.make_async_remote_copy(
                src_ref=fwd_out.at[:, cols],
                dst_ref=hid.at[:, cols],
                send_sem=hop_send.at[0],
                recv_sem=hop_recv.at[0],
                device_id={"section": wrap(section + 1)},
                device_id_type=MESH,
            ).start()
            return carry

        lax.fori_loop(0, WIDTH // TILE, out_tile, 0)

    for there in range(RING):
        for block in range(RING):
            n_send_buf[there, :, block * 128 : (block + 1) * 128] = normed[
                :, (block * RING + there) * 128 : (block * RING + there + 1) * 128
            ]
    n_trade = Exchange(place, "y", lambda there: n_send_buf.at[there], n_all, n_send, n_recv)
    n_all[place.y] = n_send_buf[place.y]
    n_trade.start()

    @pl.when(section < last)
    def _():
        pltpu.make_async_remote_copy(
            src_ref=up,
            dst_ref=up,
            send_sem=hop_send.at[1],
            recv_sem=hop_recv.at[1],
            device_id={"section": wrap(section + 1)},
            device_id_type=MESH,
        ).wait_recv()

    def mixed_tile(j, carry):
        cols = pl.ds(pl.multiple_of(j * TILE, TILE), TILE)
        mixed_grad[:, cols] = mm(up[...], wo[cols, :], NT).astype(BF)
        return carry

    lax.fori_loop(0, QW // TILE, mixed_tile, 0)

    k_mine = k_all.at[place.y]
    low = lower_lanes((TOKENS, 128))
    folded = []
    for group in range(4):
        start = (group // 2) * 128
        keys = both_halves(kv[:, start : start + 128], group % 2)
        values = both_halves(kv[:, 256 + start : 256 + start + 128], group % 2)
        heads = head_rows(q, group)
        heads_grad = head_rows(mixed_grad, group)
        prob = probs[group]
        prob_grad = mm(heads_grad, values, NT)
        inner = jnp.sum(prob_grad * prob, axis=-1, keepdims=True)
        score_grad = (prob * (prob_grad - inner) * (HEAD**-0.5)).astype(BF)
        put_heads(dq, group, mm(score_grad, keys))
        dk = mm(score_grad, heads, TN)
        dv = mm(prob.astype(BF), heads_grad, TN)
        folded.append((dk + pltpu.roll(dk, HEAD, 1), dv + pltpu.roll(dv, HEAD, 1)))
        if group % 2 == 1:
            for part in range(2):
                both = jnp.where(low, folded[group - 1][part], folded[group][part]).astype(BF)
                k_mine[:, part * 256 + start : part * 256 + start + 128] = both

    k_trade = Exchange(place, "y", lambda there: k_mine, k_all, k_send, k_recv)
    k_trade.start()

    @pl.when(section > 0)
    def _():
        def grad_tile(j, total):
            cols = pl.ds(pl.multiple_of(j * TILE, TILE), TILE)
            part = mm(dq[...], wq[cols, :], NT)
            first = mm(k_mine[:HALF, :], kv_stash[0, cols, :], NT)
            second = mm(k_mine[HALF:, :], kv_now[0, cols, :], NT)
            part = part + jnp.concatenate([first, second], axis=0)
            part = part * gain[:, cols].astype(F32)
            dnormed[:, cols] = part
            dot = part * hid[:, cols].astype(F32)
            return total + dot[:, :128] + dot[:, 128:]

        total = lax.fori_loop(0, WIDTH // TILE, grad_tile, jnp.zeros((TOKENS, 128), F32))
        r = scale[:, :1]
        inner = jnp.sum(total, axis=-1, keepdims=True) * (r * r * r) * (1.0 / WIDTH)

        def out_tile(j, carry):
            cols = pl.ds(pl.multiple_of(j * TILE, TILE), TILE)
            through = dnormed[:, cols] * r - hid[:, cols].astype(F32) * inner
            bwd_out[:, cols] = (up[:, cols].astype(F32) + through).astype(BF)
            pltpu.make_async_remote_copy(
                src_ref=bwd_out.at[:, cols],
                dst_ref=up.at[:, cols],
                send_sem=hop_send.at[1],
                recv_sem=hop_recv.at[1],
                device_id={"section": wrap(section - 1)},
                device_id_type=MESH,
            ).start()
            return carry

        lax.fori_loop(0, WIDTH // TILE, out_tile, 0)

    n_trade.wait()
    k_trade.wait()

    for step in range(2):
        tokens = slice(step * HALF, (step + 1) * HALF)
        right = k_all[:, tokens, :].reshape(RING * HALF, KVW)
        for block in range(RING):
            left = n_all[:, tokens, block * 128 : (block + 1) * 128].reshape(RING * HALF, 128)
            part = mm(left, right, TN).astype(BF)
            for there in range(RING):
                x_buf[there, block, :, step * KVW : (step + 1) * KVW] = part[
                    there * 32 : (there + 1) * 32
                ]

    x_trade = Exchange(place, "x", lambda there: x_buf.at[there], x_all, x_send, x_recv)
    x_all[place.x] = x_buf[place.x]
    x_trade.start()
    x_trade.wait()
    for block in range(RING):
        total = x_all[0, block].astype(F32)
        for there in range(1, RING):
            total = total + x_all[there, block].astype(F32)
        z_buf[block] = total.astype(BF)
    z_trade = Exchange(place, "z", lambda there: z_buf.at[there], z_all, z_send, z_recv)
    z_all[place.z] = z_buf[place.z]
    z_trade.start()
    z_trade.wait()
    grads = z_all[0].astype(F32)
    for there in range(1, RING):
        grads = grads + z_all[there].astype(F32)
    grads = grads * (1.0 / REPLICAS)

    stash_all, next_all = stash_out.at[0], next_out.at[0]
    outputs = Gather(
        place, [(stash_all, 32, ("x", "y")), (next_all, 32, ("y", "x"))], o_send, o_recv
    )
    own = pl.ds(pl.multiple_of(place.me * 32, 32), 32)
    rows = kv_now[0, own, :]
    first, second = adam_m[0], adam_v[0]
    for step, target in ((0, stash_all), (1, next_all)):
        grad = grads[:, step * KVW : (step + 1) * KVW]
        first_new = beta_first * first.astype(F32) + (1.0 - beta_first) * grad
        second_new = beta_second * second.astype(F32) + (1.0 - beta_second) * grad * grad
        moved = rows.astype(F32) - learn_rate * first_new / (jnp.sqrt(second_new) + adam_eps)
        rows, first, second = moved.astype(BF), first_new.astype(BF), second_new.astype(BF)
        target[own, :] = rows
    m_out[0] = first
    v_out[0] = second
    outputs.begin()
    outputs.finish()

    weights.drain()
    outputs.drain()

    @pl.when(section < last)
    def _():
        pltpu.make_async_remote_copy(
            src_ref=fwd_out,
            dst_ref=hid,
            send_sem=hop_send.at[0],
            recv_sem=hop_recv.at[0],
            device_id={"section": wrap(section + 1)},
            device_id_type=MESH,
        ).wait_send()

    @pl.when(section > 0)
    def _():
        pltpu.make_async_remote_copy(
            src_ref=bwd_out,
            dst_ref=up,
            send_sem=hop_send.at[1],
            recv_sem=hop_recv.at[1],
            device_id={"section": wrap(section - 1)},
            device_id_type=MESH,
        ).wait_send()


def body(
    embeddings, cotangent, plan, doc_ids, norm_gain, w_query, w_out, kv_stash, kv_now, adam_m, adam_v
):
    docs = doc_ids[0][plan[0]] + 8 * jnp.arange(4, dtype=jnp.int32)[:, None]
    docs = docs.reshape(TOKENS)
    places = jnp.arange(TOKENS)
    mask = (docs[:, None] == docs[None, :]) & (places[:, None] >= places[None, :])
    mask = mask.astype(F32)
    vmem = pl.BlockSpec(memory_space=pltpu.VMEM)
    smem = pl.BlockSpec(memory_space=pltpu.SMEM)
    dma = pltpu.SemaphoreType.DMA
    version = jax.ShapeDtypeStruct((1, WIDTH, KVW), BF)
    moment = jax.ShapeDtypeStruct((1, 32, KVW), BF)
    return pl.pallas_call(
        kernel,
        out_shape=(version, version, moment, moment),
        in_specs=[vmem, vmem, smem] + [vmem] * 8,
        out_specs=(vmem,) * 4,
        scratch_shapes=[
            pltpu.VMEM((WIDTH, QW), BF),
            pltpu.VMEM((QW, WIDTH), BF),
            pltpu.VMEM((TOKENS, WIDTH), BF),
            pltpu.VMEM((TOKENS, WIDTH), BF),
            pltpu.VMEM((TOKENS, WIDTH), BF),
            pltpu.VMEM((TOKENS, WIDTH), BF),
            pltpu.VMEM((TOKENS, WIDTH), BF),
            pltpu.VMEM((TOKENS, 128), F32),
            pltpu.VMEM((TOKENS, QW), BF),
            pltpu.VMEM((TOKENS, KVW), BF),
            pltpu.VMEM((4, 4 * TOKENS, TOKENS), F32),
            pltpu.VMEM((TOKENS, QW), BF),
            pltpu.VMEM((TOKENS, QW), BF),
            pltpu.VMEM((TOKENS, QW), BF),
            pltpu.VMEM((TOKENS, WIDTH), F32),
            pltpu.VMEM((RING, TOKENS, 512), BF),
            pltpu.VMEM((RING, TOKENS, 512), BF),
            pltpu.VMEM((RING, TOKENS, KVW), BF),
            pltpu.VMEM((RING, RING, 32, 2 * KVW), BF),
            pltpu.VMEM((RING, RING, 32, 2 * KVW), BF),
            pltpu.VMEM((RING, 32, 2 * KVW), BF),
            pltpu.VMEM((RING, 32, 2 * KVW), BF),
            dma((2,)),
            dma((2, REPLICAS)),
            dma((2,)),
            dma((2, REPLICAS)),
            dma((2,)),
            dma((2,)),
            dma((3,)),
            dma((3,)),
            dma((3,)),
            dma((3,)),
            dma((3,)),
            dma((3,)),
            dma((3,)),
            dma((3,)),
        ],
        compiler_params=pltpu.CompilerParams(
            collective_id=0, has_side_effects=True, vmem_limit_bytes=56 * 1024 * 1024
        ),
    )(embeddings, cotangent, plan, mask, norm_gain, w_query, w_out, kv_stash, kv_now, adam_m, adam_v)


def solution(mesh):
    placed = (
        P("replica", None, None, None),
        P("replica", None, None, None),
        P("replica", None),
        P("replica", None, None),
        P("section", None),
        P("section", "replica", None),
        P("section", "replica", None),
        P("section", None, None),
        P("section", None, None),
        P("section", "replica", None),
        P("section", "replica", None),
    )
    return jax.shard_map(
        body,
        mesh=mesh,
        in_specs=placed,
        out_specs=(
            P("section", None, None),
            P("section", None, None),
            P("section", "replica", None),
            P("section", "replica", None),
        ),
        check_vma=False,
    )
```

```python
import functools

import jax
import jax.numpy as jnp
from jax import lax
from jax.experimental import pallas as pl
from jax.experimental.pallas import tpu as pltpu
from jax.sharding import PartitionSpec as P

HEAD = 64
RING = 4
REPLICAS = 64
TOKENS = 128
HALF = 64
WIDTH = 2048
QW = 1024
KVW = 512
WIDE = 512
CHUNKS = 4
BF = jnp.bfloat16
F32 = jnp.float32
MESH = pl.DeviceIdType.MESH

beta_first = 0.9
beta_second = 0.999
learn_rate = 0.003
adam_eps = 1e-08
norm_eps = 1e-05

NN = (((1,), (0,)), ((), ()))
NT = (((1,), (1,)), ((), ()))
TN = (((0,), (0,)), ((), ()))


def mm(a, b, dims=NN):
    return lax.dot_general(a, b, dims, preferred_element_type=F32)


def wrap(v):
    return lax.rem(v + RING, RING)


class Place:
    def __init__(self):
        me = lax.axis_index("replica")
        self.me = me
        self.z = me // 16
        self.y = lax.rem(me // 4, RING)
        self.x = lax.rem(me, RING)
        self.line = {}
        for axis, own in (("z", self.z), ("y", self.y), ("x", self.x)):
            self.line[axis] = [own] + [wrap(own + step) for step in range(1, RING)]

    def on(self, axis, step):
        return self.line[axis][step % RING]

    def at(self, axis, step):
        spot = {"z": self.z, "y": self.y, "x": self.x}
        spot[axis] = self.on(axis, step)
        return (spot["z"] * RING + spot["y"]) * RING + spot["x"]


class Gather:
    def __init__(self, place, parts, send, recv, direct, far):
        self.place, self.parts, self.send, self.recv = place, parts, send, recv
        self.direct, self.far = direct, far
        self.peer = {
            (axis, step): place.at(axis, step) for axis in ("x", "y", "z") for step in (1, -1, 2)
        }

    def piece(self, k, dz, du=0, dv=0, many=None):
        ref, first, columns, u, v = self.parts[k]
        spot = {u: self.place.on(u, du), v: self.place.on(v, dv)}
        if many is not None:
            spot[u] = many
        return ref.at[self.place.on("z", dz), spot["y"], spot["x"], :, pl.ds(first, columns)]

    def copy(self, k, piece, axis, step, slot):
        stage = 0 if slot < 3 else 1 if slot < 15 else 2
        return pltpu.make_async_remote_copy(
            src_ref=piece,
            dst_ref=piece,
            send_sem=self.send.at[k, stage],
            recv_sem=self.recv.at[k, slot],
            device_id={"replica": self.peer[axis, step]},
            device_id_type=MESH,
        )

    def along_z(self, k, start):
        for step in (1, -1):
            copy = self.copy(k, self.piece(k, 0 if start else -step), "z", step, (1 - step) // 2)
            copy.start() if start else copy.wait_recv()

    def past_z(self, k, start):
        step = 1 if k % 2 else -1
        source = -step
        if self.far:
            step, source = 2, 0
        copy = self.copy(k, self.piece(k, source if start else 2), "z", step, 2)
        copy.start() if start else copy.wait_recv()

    def along_u(self, k, dz, start):
        u = self.parts[k][3]
        for step in (1, -1):
            piece = self.piece(k, dz, 0 if start else -step)
            copy = self.copy(k, piece, u, step, 3 + 3 * (dz % RING) + (1 - step) // 2)
            copy.start() if start else copy.wait_recv()

    def past_u(self, k, dz, start):
        u = self.parts[k][3]
        step = 1 if dz % 2 else -1
        source = -step
        if dz % RING in self.direct:
            step, source = 2, 0
        piece = self.piece(k, dz, source if start else 2)
        copy = self.copy(k, piece, u, step, 3 + 3 * (dz % RING) + 2)
        copy.start() if start else copy.wait_recv()

    def along_v(self, k, dz, start):
        v = self.parts[k][4]
        for step in (1, -1):
            piece = self.piece(k, dz, 0, 0 if start else -step, slice(0, RING))
            copy = self.copy(k, piece, v, step, 15 + 4 * (dz % RING) + (1 - step) // 2)
            copy.start() if start else copy.wait_recv()

    def past_v(self, k, dz, start):
        v = self.parts[k][4]
        for step in (1, -1):
            half = slice(0, 2) if step == 1 else slice(2, RING)
            piece = self.piece(k, dz, 0, -step if start else 2, half)
            copy = self.copy(k, piece, v, step, 17 + 4 * (dz % RING) + (1 - step) // 2)
            copy.start() if start else copy.wait_recv()

    def send_u(self, k, dz):
        self.along_u(k, dz, True)
        if dz % RING in self.direct:
            self.past_u(k, dz, True)

    def take_u(self, k, dz):
        self.along_u(k, dz, False)
        if dz % RING not in self.direct:
            self.past_u(k, dz, True)

    def send_v(self, k, dz):
        self.past_u(k, dz, False)
        self.along_v(k, dz, True)

    def take_v(self, k, dz):
        self.along_v(k, dz, False)
        self.past_v(k, dz, True)

    def begin(self, parts):
        for k in parts:
            self.along_z(k, True)
        for k in parts:
            self.send_u(k, 0)
        for k in parts:
            if self.far:
                self.past_z(k, True)

    def finish(self, parts):
        def each(step, *planes):
            for dz in planes:
                for k in parts:
                    step(k, dz)

        each(self.take_u, 0)
        each(self.send_v, 0)
        for k in parts:
            self.along_z(k, False)
            if not self.far:
                self.past_z(k, True)
        each(self.send_u, -1, 1)
        each(self.take_u, -1, 1)
        each(self.take_v, 0)
        for k in parts:
            self.past_z(k, False)
        each(self.send_u, 2)
        each(self.send_v, -1, 1)
        each(self.take_u, 2)
        each(self.send_v, 2)
        each(self.take_v, -1, 1, 2)
        each(lambda k, dz: self.past_v(k, dz, False), 0, -1, 1, 2)

    def drain(self):
        for k in range(len(self.parts)):
            ref, first, columns = self.parts[k][:3]
            columns = pl.ds(first, columns)
            sent = (
                ref.at[0, 0, 0:3, :, columns],
                ref.at[0, 0:3, :, :, columns],
                ref.at[0:3, :, :, :, columns],
            )
            for piece, slot in zip(sent, (0, 3, 15)):
                self.copy(k, piece, "x", 1, slot).wait_send()


class Exchange:
    def __init__(self, place, axis, out, into, send, recv):
        self.place, self.axis, self.out, self.into = place, axis, out, into
        self.send, self.recv = send, recv
        self.mine = {"x": place.x, "y": place.y, "z": place.z}[axis]

    def copies(self):
        for step in (1, 3, 2):
            there = self.place.on(self.axis, step)
            source = self.out(there)
            yield there, step, pltpu.make_async_remote_copy(
                src_ref=source,
                dst_ref=self.into.at[self.mine],
                send_sem=self.send.at[step - 1],
                recv_sem=self.recv.at[step - 1],
                device_id={"replica": self.place.at(self.axis, step)},
                device_id_type=MESH,
            )

    def start(self):
        for there, step, copy in self.copies():
            copy.start()

    def wait(self):
        for there, step, copy in self.copies():
            copy.wait_recv()
        for there, step, copy in self.copies():
            copy.wait_send()


def lower_lanes(shape):
    return lax.broadcasted_iota(jnp.int32, shape, len(shape) - 1) < HEAD


def both_halves(block, half):
    low = lower_lanes(block.shape)
    wide = block.astype(F32)
    own = jnp.where(low, wide, 0.0) if half == 0 else jnp.where(low, 0.0, wide)
    return (own + pltpu.roll(own, HEAD, 1)).astype(BF)


def head_rows(ref, group):
    blocks = []
    for j in range(4):
        start = (2 * group + j // 2) * 128
        block = ref[:, start : start + 128]
        low = lower_lanes(block.shape)
        zero = jnp.zeros_like(block)
        blocks.append(jnp.where(low, block, zero) if j % 2 == 0 else jnp.where(low, zero, block))
    return jnp.concatenate(blocks, axis=0)


def put_heads(ref, group, rows):
    low = lower_lanes((TOKENS, 128))
    for b in range(2):
        first = rows[2 * b * TOKENS : (2 * b + 1) * TOKENS]
        second = rows[(2 * b + 1) * TOKENS : (2 * b + 2) * TOKENS]
        start = (2 * group + b) * 128
        ref[:, start : start + 128] = jnp.where(low, first, second).astype(BF)


def kernel(
    emb_in,
    cot_in,
    plan,
    docs,
    gain,
    wq_share,
    wo_share,
    stash_in,
    now_in,
    adam_m,
    adam_v,
    stash_out,
    next_out,
    m_out,
    v_out,
    emb,
    cot,
    kv_stash,
    kv_now,
    tags,
    wq,
    wo,
    wq_t,
    wo_t,
    stash_t,
    now_t,
    hid,
    up,
    fwd_out,
    bwd_out,
    wide,
    scale,
    q,
    kv,
    probs,
    mixed,
    mixed_grad,
    dq,
    kg,
    n_t,
    n_y,
    n_x,
    k_y,
    k_x,
    x_buf,
    x_all,
    y_buf,
    y_all,
    z_buf,
    z_all,
    w_send,
    w_recv,
    o_send,
    o_recv,
    hop_send,
    hop_recv,
    trade_send,
    trade_recv,
    load_sem,
):
    place = Place()
    section = lax.axis_index("section")
    last = RING - 1

    loads = [
        pltpu.make_async_copy(src, dst, load_sem.at[i])
        for i, (src, dst) in enumerate(
            ((emb_in, emb), (cot_in, cot), (stash_in, kv_stash), (now_in, kv_now))
        )
    ]
    for load in loads:
        load.start()

    def load_wait():
        for load in loads:
            load.wait()

    barrier = pltpu.get_barrier_semaphore()
    for axis in ("x", "y", "z"):
        for step in (1, 2, 3):
            pl.semaphore_signal(
                barrier, inc=1, device_id={"replica": place.at(axis, step)}, device_id_type=MESH
            )
    for step in (1, -1):
        pl.semaphore_signal(
            barrier, inc=1, device_id={"section": wrap(section + step)}, device_id_type=MESH
        )
    pl.semaphore_wait(barrier, 11)

    def columns(c, size=WIDE):
        return slice(c * size, (c + 1) * size)

    def hop(way, src, dst, c, to):
        return pltpu.make_async_remote_copy(
            src_ref=src.at[:, columns(c)],
            dst_ref=dst.at[:, columns(c)],
            send_sem=hop_send.at[way, c],
            recv_sem=hop_recv.at[way, c],
            device_id={"section": wrap(section + to)},
            device_id_type=MESH,
        )

    def drain_hops():
        @pl.when(section < last)
        def _():
            for c in range(CHUNKS):
                hop(0, fwd_out, hid, c, 1).wait_send()

        @pl.when(section > 0)
        def _():
            for c in range(CHUNKS):
                hop(1, bwd_out, up, c, -1).wait_send()

    def four(block):
        return block[:, :128] + block[:, 128:256] + block[:, 256:384] + block[:, 384:]

    def allowed():
        tag = jnp.broadcast_to(tags[:1, :], (TOKENS, TOKENS))
        row = lax.broadcasted_iota(jnp.int32, (TOKENS, TOKENS), 0)
        col = lax.broadcasted_iota(jnp.int32, (TOKENS, TOKENS), 1)
        return (tag == tag.T) & (row // 32 == col // 32) & (row >= col)

    def project():
        @pl.when(section == 0)
        def _():
            for i in range(RING):
                hid[i * 32 : (i + 1) * 32, :] = emb[0, plan[0, i]]

        for c in range(CHUNKS):
            cols = columns(c)

            @pl.when(section > 0)
            def _():
                hop(0, fwd_out, hid, c, -1).wait_recv()

            own = hid[:, cols].astype(F32)
            gained = (own * gain[:, cols].astype(F32)).astype(BF)
            squares = four(own * own)
            products = (
                mm(gained, wq[c].reshape(WIDE, QW)),
                mm(gained[:HALF], kv_stash[0, cols, :]),
                mm(gained[HALF:], kv_now[0, cols, :]),
            )
            if c == 0:
                wide[:, :QW] = products[0]
                wide[:HALF, QW : QW + KVW] = products[1]
                wide[HALF:, QW : QW + KVW] = products[2]
                scale[...] = squares
            else:
                wide[:, :QW] += products[0]
                wide[:HALF, QW : QW + KVW] += products[1]
                wide[HALF:, QW : QW + KVW] += products[2]
                scale[...] += squares
        mean = jnp.sum(scale[...], axis=-1, keepdims=True) * (1.0 / WIDTH)
        r = lax.rsqrt(mean + norm_eps)
        scale[...] = jnp.broadcast_to(r, (TOKENS, 128))
        q[...] = (wide[:, :QW] * r).astype(BF)
        kv[...] = (wide[:, QW : QW + KVW] * r).astype(BF)

        mask = allowed()
        for group in range(4):
            start = (group // 2) * 128
            keys = both_halves(kv[:, start : start + 128], group % 2)
            values = both_halves(kv[:, 256 + start : 256 + start + 128], group % 2)
            score = mm(head_rows(q, group), keys, NT).reshape(4, TOKENS, TOKENS)
            weight = jnp.where(mask[None], jnp.exp(score * (HEAD**-0.5)), 0.0)
            prob = weight / jnp.sum(weight, axis=-1, keepdims=True)
            prob = prob.reshape(4 * TOKENS, TOKENS)
            probs[group] = prob

            @pl.when(section < last)
            def _():
                put_heads(mixed, group, mm(prob.astype(BF), values))

    def prepare():
        def turn(i, carry):
            rows = pl.ds(pl.multiple_of(i * WIDE, WIDE), WIDE)
            wq_t[:, rows] = wq[i].reshape(WIDE, QW).T
            stash_t[:, rows] = kv_stash[0, rows, :].T
            now_t[:, rows] = kv_now[0, rows, :].T
            return carry

        def turn_out(i, carry):
            rows = pl.ds(pl.multiple_of(i * 256, 256), 256)
            wo_t[:, rows] = wo[i].reshape(256, WIDTH).T
            return carry

        lax.fori_loop(0, RING, turn_out, 0)
        lax.fori_loop(0, RING, turn, 0)

    def trade(index, axis, out, into):
        return Exchange(place, axis, out, into, trade_send.at[index], trade_recv.at[index])

    n_trades = (
        trade(0, "y", lambda there: n_t.at[0:2, there], n_y),
        trade(1, "x", lambda there: n_t.at[2:4, :, there], n_x),
    )
    k_trades = (trade(2, "y", lambda there: kg, k_y), trade(3, "x", lambda there: kg, k_x))

    def share_normed():
        for block in range(RING * RING):
            cols = columns(block, 128)
            own = hid[:, cols].astype(F32) * scale[...] * gain[:, cols].astype(F32)
            n_t[block // RING, block % RING] = own.astype(BF).T.reshape(RING, 32, TOKENS)
        n_y[place.y] = n_t[0:2, place.y]
        n_x[place.x] = n_t[2:4, :, place.x]
        for one in n_trades:
            one.start()

    def make_mixed_grad(streamed):
        for c in range(CHUNKS):
            if streamed:
                hop(1, bwd_out, up, c, 1).wait_recv()
            part = mm(up[:, columns(c)], wo_t[columns(c), :])
            if c == 0:
                wide[:, :QW] = part
            elif c < CHUNKS - 1:
                wide[:, :QW] += part
            else:
                mixed_grad[...] = (wide[:, :QW] + part).astype(BF)

    weights = Gather(
        place,
        [
            (wq, 0, QW // 2, "x", "y"),
            (wq, QW // 2, QW // 2, "y", "x"),
            (wo, 0, WIDTH // 2, "x", "y"),
            (wo, WIDTH // 2, WIDTH // 2, "y", "x"),
        ],
        w_send,
        w_recv,
        (),
        False,
    )
    wq[place.z, place.y, place.x] = wq_share[0]
    wo[place.z, place.y, place.x] = wo_share[0]

    weights.begin((0, 1, 2, 3))
    for i in range(RING):
        tags[:1, i * 32 : (i + 1) * 32] = docs[0, pl.ds(plan[0, i], 1), :].astype(F32)
    weights.finish((0, 1, 2, 3))

    load_wait()

    @pl.when(section == last)
    def _():
        prepare()
        for i in range(RING):
            up[i * 32 : (i + 1) * 32, :] = cot[0, plan[0, i]]
        make_mixed_grad(False)

    project()

    @pl.when(section < last)
    def _():
        for c in range(CHUNKS):
            cols = columns(c)
            fwd_out[:, cols] = (hid[:, cols].astype(F32) + mm(mixed[...], wo[:, :, :, :, cols].reshape(QW, WIDE))).astype(BF)
            hop(0, fwd_out, hid, c, 1).start()
        prepare()
        share_normed()
        make_mixed_grad(True)

    low = lower_lanes((TOKENS, 128))
    folded = []
    for group in range(4):
        start = (group // 2) * 128
        keys = both_halves(kv[:, start : start + 128], group % 2)
        values = both_halves(kv[:, 256 + start : 256 + start + 128], group % 2)
        heads = head_rows(q, group)
        heads_grad = head_rows(mixed_grad, group)
        prob = probs[group]
        prob_grad = mm(heads_grad, values, NT)
        inner = jnp.sum(prob_grad * prob, axis=-1, keepdims=True)
        score_grad = (prob * (prob_grad - inner) * (HEAD**-0.5)).astype(BF)
        put_heads(dq, group, mm(score_grad, keys))
        dk = mm(score_grad, heads, TN)
        dv = mm(prob.astype(BF), heads_grad, TN)
        folded.append((dk + pltpu.roll(dk, HEAD, 1), dv + pltpu.roll(dv, HEAD, 1)))
        if group % 2 == 1:
            for part in range(2):
                both = jnp.where(low, folded[group - 1][part], folded[group][part]).astype(BF)
                kg[:, part * 256 + start : part * 256 + start + 128] = both

    k_y[place.y] = kg[...]
    k_x[place.x] = kg[...]
    for one in k_trades:
        one.start()

    @pl.when(section > 0)
    def _():
        total = jnp.zeros((TOKENS, 128), F32)
        for c in range(CHUNKS):
            cols = columns(c)
            first = mm(kg[:HALF, :], stash_t[:, cols])
            second = mm(kg[HALF:, :], now_t[:, cols])
            part = mm(dq[...], wq_t[:, cols]) + jnp.concatenate([first, second], axis=0)
            part = part * gain[:, cols].astype(F32)
            wide[:, cols] = part
            total = total + four(part * hid[:, cols].astype(F32))
        r = scale[...]
        inner = jnp.sum(total, axis=-1, keepdims=True) * (1.0 / WIDTH)
        inner = jnp.broadcast_to(inner, (TOKENS, 128)) * (r * r * r)
        for c in range(CHUNKS):
            for d in range(RING):
                cols = columns(c * RING + d, 128)
                through = wide[:, cols] * r - hid[:, cols].astype(F32) * inner
                bwd_out[:, cols] = (up[:, cols].astype(F32) + through).astype(BF)
            hop(1, bwd_out, up, c, -1).start()

    @pl.when(section == last)
    def _():
        share_normed()

    for one in n_trades + k_trades:
        one.wait()
    token = lax.broadcasted_iota(jnp.int32, (256, RING * TOKENS), 1)
    early = lax.rem(token, TOKENS) < HALF
    for n_all, k_all, buf in ((n_y, k_y, x_buf), (n_x, k_x, y_buf)):
        left = jnp.concatenate([n_all[src].reshape(256, TOKENS) for src in range(RING)], axis=1)
        right = k_all[...].reshape(RING * TOKENS, KVW)
        zero = jnp.zeros_like(left)
        for step in range(2):
            own = jnp.where(early, left, zero) if step == 0 else jnp.where(early, zero, left)
            part = mm(own, right).astype(BF).reshape(2, RING, 32, KVW)
            for there in range(RING):
                buf[there, :, :, step * KVW : (step + 1) * KVW] = part[:, there]
        one = (
            trade(4, "x", lambda there: x_buf.at[there], x_all)
            if buf is x_buf
            else trade(5, "y", lambda there: y_buf.at[there], y_all)
        )
        one.start()
    x_all[place.x] = x_buf[place.x]
    y_all[place.y] = y_buf[place.y]
    trade(4, "x", lambda there: x_buf.at[there], x_all).wait()
    trade(5, "y", lambda there: y_buf.at[there], y_all).wait()
    for start, parts in ((0, x_all), (2, y_all)):
        total = parts[0].astype(F32)
        for src in range(1, RING):
            total = total + parts[src].astype(F32)
        z_buf[start : start + 2] = total.astype(BF)
    z_trade = trade(6, "z", lambda there: z_buf.at[there], z_all)
    z_all[place.z] = z_buf[place.z]
    z_trade.start()
    z_trade.wait()
    grads = z_all[0].astype(F32)
    for src in range(1, RING):
        grads = grads + z_all[src].astype(F32)
    grads = grads * (1.0 / REPLICAS)
    outputs = Gather(
        place, [(stash_out, 0, KVW, "x", "y"), (next_out, 0, KVW, "y", "x")], o_send, o_recv, (0, 1, 2, 3), True
    )
    own = pl.ds(pl.multiple_of(place.me * 32, 32), 32)
    rows = kv_now[0, own, :]
    first, second = adam_m[0], adam_v[0]
    for step, target in ((0, stash_out), (1, next_out)):
        grad = grads[:, step * KVW : (step + 1) * KVW]
        first_new = beta_first * first.astype(F32) + (1.0 - beta_first) * grad
        second_new = beta_second * second.astype(F32) + (1.0 - beta_second) * grad * grad
        moved = rows.astype(F32) - learn_rate * first_new / (jnp.sqrt(second_new) + adam_eps)
        rows, first, second = moved.astype(BF), first_new.astype(BF), second_new.astype(BF)
        target[place.z, place.y, place.x] = rows
        outputs.begin((step,))
    m_out[0] = first
    v_out[0] = second
    outputs.finish((0, 1))

    weights.drain()
    outputs.drain()
    drain_hops()


def body(
    embeddings, cotangent, plan, doc_ids, norm_gain, w_query, w_out, kv_stash, kv_now, adam_m, adam_v
):
    vmem = pl.BlockSpec(memory_space=pltpu.VMEM)
    smem = pl.BlockSpec(memory_space=pltpu.SMEM)
    hbm = pl.BlockSpec(memory_space=pl.ANY)
    dma = pltpu.SemaphoreType.DMA
    version = jax.ShapeDtypeStruct((RING, RING, RING, 32, KVW), BF)
    moment = jax.ShapeDtypeStruct((1, 32, KVW), BF)
    stash, current, first, second = pl.pallas_call(
        kernel,
        out_shape=(version, version, moment, moment),
        in_specs=[hbm, hbm, smem, vmem, vmem, vmem, vmem, hbm, hbm, vmem, vmem],
        out_specs=(vmem,) * 4,
        scratch_shapes=[
            pltpu.VMEM((1, 4, 32, WIDTH), BF),
            pltpu.VMEM((1, 4, 32, WIDTH), BF),
            pltpu.VMEM((1, WIDTH, KVW), BF),
            pltpu.VMEM((1, WIDTH, KVW), BF),
            pltpu.VMEM((8, TOKENS), F32),
            pltpu.VMEM((RING, RING, RING, 32, QW), BF),
            pltpu.VMEM((RING, RING, RING, 16, WIDTH), BF),
            pltpu.VMEM((QW, WIDTH), BF),
            pltpu.VMEM((WIDTH, QW), BF),
            pltpu.VMEM((KVW, WIDTH), BF),
            pltpu.VMEM((KVW, WIDTH), BF),
            pltpu.VMEM((TOKENS, WIDTH), BF),
            pltpu.VMEM((TOKENS, WIDTH), BF),
            pltpu.VMEM((TOKENS, WIDTH), BF),
            pltpu.VMEM((TOKENS, WIDTH), BF),
            pltpu.VMEM((TOKENS, WIDTH), F32),
            pltpu.VMEM((TOKENS, 128), F32),
            pltpu.VMEM((TOKENS, QW), BF),
            pltpu.VMEM((TOKENS, KVW), BF),
            pltpu.VMEM((4, 4 * TOKENS, TOKENS), F32),
            pltpu.VMEM((TOKENS, QW), BF),
            pltpu.VMEM((TOKENS, QW), BF),
            pltpu.VMEM((TOKENS, QW), BF),
            pltpu.VMEM((TOKENS, KVW), BF),
            pltpu.VMEM((RING, RING, RING, 32, TOKENS), BF),
            pltpu.VMEM((RING, 2, RING, 32, TOKENS), BF),
            pltpu.VMEM((RING, 2, RING, 32, TOKENS), BF),
            pltpu.VMEM((RING, TOKENS, KVW), BF),
            pltpu.VMEM((RING, TOKENS, KVW), BF),
            pltpu.VMEM((RING, 2, 32, 2 * KVW), BF),
            pltpu.VMEM((RING, 2, 32, 2 * KVW), BF),
            pltpu.VMEM((RING, 2, 32, 2 * KVW), BF),
            pltpu.VMEM((RING, 2, 32, 2 * KVW), BF),
            pltpu.VMEM((RING, 32, 2 * KVW), BF),
            pltpu.VMEM((RING, 32, 2 * KVW), BF),
            dma((4, 3)),
            dma((4, 31)),
            dma((2, 3)),
            dma((2, 31)),
            dma((2, CHUNKS)),
            dma((2, CHUNKS)),
            dma((7, RING - 1)),
            dma((7, RING - 1)),
            dma((4,)),
        ],
        compiler_params=pltpu.CompilerParams(
            collective_id=0, has_side_effects=True, vmem_limit_bytes=56 * 1024 * 1024
        ),
    )(embeddings, cotangent, plan, doc_ids, norm_gain, w_query, w_out, kv_stash, kv_now, adam_m, adam_v)
    shape = (1, WIDTH, KVW)
    return stash.reshape(shape), current.reshape(shape), first, second


def solution(mesh):
    placed = (
        P("replica", None, None, None),
        P("replica", None, None, None),
        P("replica", None),
        P("replica", None, None),
        P("section", None),
        P("section", "replica", None),
        P("section", "replica", None),
        P("section", None, None),
        P("section", None, None),
        P("section", "replica", None),
        P("section", "replica", None),
    )
    return jax.shard_map(
        body,
        mesh=mesh,
        in_specs=placed,
        out_specs=(
            P("section", None, None),
            P("section", None, None),
            P("section", "replica", None),
            P("section", "replica", None),
        ),
        check_vma=False,
    )
```

```python
import functools

import jax
import jax.numpy as jnp
from jax import lax
from jax.experimental import pallas as pl
from jax.experimental.pallas import tpu as pltpu
from jax.sharding import PartitionSpec as P

HEAD = 64
RING = 4
REPLICAS = 64
TOKENS = 128
HALF = 64
WIDTH = 2048
QW = 1024
KVW = 512
WIDE = 512
CHUNKS = 4
BF = jnp.bfloat16
F32 = jnp.float32
MESH = pl.DeviceIdType.MESH

beta_first = 0.9
beta_second = 0.999
learn_rate = 0.003
adam_eps = 1e-08
norm_eps = 1e-05

NN = (((1,), (0,)), ((), ()))
NT = (((1,), (1,)), ((), ()))
TN = (((0,), (0,)), ((), ()))


def mm(a, b, dims=NN):
    return lax.dot_general(a, b, dims, preferred_element_type=F32)


def wrap(v):
    return lax.rem(v + RING, RING)


class Place:
    def __init__(self):
        me = lax.axis_index("replica")
        self.me = me
        self.z = me // 16
        self.y = lax.rem(me // 4, RING)
        self.x = lax.rem(me, RING)
        self.line = {}
        for axis, own in (("z", self.z), ("y", self.y), ("x", self.x)):
            self.line[axis] = [own] + [wrap(own + step) for step in range(1, RING)]

    def on(self, axis, step):
        return self.line[axis][step % RING]

    def at(self, axis, step):
        spot = {"z": self.z, "y": self.y, "x": self.x}
        spot[axis] = self.on(axis, step)
        return (spot["z"] * RING + spot["y"]) * RING + spot["x"]


class Gather:
    def __init__(self, place, parts, send, recv, direct, far, over):
        self.place, self.parts, self.send, self.recv = place, parts, send, recv
        self.direct, self.far, self.over = direct, far, over
        self.peer = {
            (axis, step): place.at(axis, step) for axis in ("x", "y", "z") for step in (1, -1, 2)
        }

    def piece(self, k, da, du=0, dv=0, many=None):
        ref, first, columns, a, u, v = self.parts[k]
        spot = {a: self.place.on(a, da), u: self.place.on(u, du), v: self.place.on(v, dv)}
        if many is not None:
            spot[u] = many
        return ref.at[spot["z"], spot["y"], spot["x"], :, pl.ds(first, columns)]

    def copy(self, k, piece, axis, step, slot):
        stage = 0 if slot < 3 else 1 if slot < 15 else 2
        return pltpu.make_async_remote_copy(
            src_ref=piece,
            dst_ref=piece,
            send_sem=self.send.at[k, stage],
            recv_sem=self.recv.at[k, slot],
            device_id={"replica": self.peer[axis, step]},
            device_id_type=MESH,
        )

    def along_a(self, k, start):
        a = self.parts[k][3]
        for step in (1, -1):
            copy = self.copy(k, self.piece(k, 0 if start else -step), a, step, (1 - step) // 2)
            copy.start() if start else copy.wait_recv()

    def past_a(self, k, start):
        a = self.parts[k][3]
        step = 1 if k % 2 else -1
        source = -step
        if self.far:
            step, source = 2, 0
        copy = self.copy(k, self.piece(k, source if start else 2), a, step, 2)
        copy.start() if start else copy.wait_recv()

    def along_u(self, k, dz, start):
        u = self.parts[k][4]
        for step in (1, -1):
            piece = self.piece(k, dz, 0 if start else -step)
            copy = self.copy(k, piece, u, step, 3 + 3 * (dz % RING) + (1 - step) // 2)
            copy.start() if start else copy.wait_recv()

    def past_u(self, k, dz, start):
        u = self.parts[k][4]
        step = 1 if dz % 2 else -1
        source = -step
        if dz % RING in self.direct:
            step, source = 2, 0
        piece = self.piece(k, dz, source if start else 2)
        copy = self.copy(k, piece, u, step, 3 + 3 * (dz % RING) + 2)
        copy.start() if start else copy.wait_recv()

    def along_v(self, k, dz, start):
        v = self.parts[k][5]
        for step in (1, -1):
            piece = self.piece(k, dz, 0, 0 if start else -step, slice(0, RING))
            copy = self.copy(k, piece, v, step, 15 + 4 * (dz % RING) + (1 - step) // 2)
            copy.start() if start else copy.wait_recv()

    def past_v(self, k, dz, start):
        v = self.parts[k][5]
        if dz % RING in self.over:
            piece = self.piece(k, dz, 0, 0 if start else 2, slice(0, RING))
            copy = self.copy(k, piece, v, 2, 17 + 4 * (dz % RING))
            copy.start() if start else copy.wait_recv()
            return
        for step in (1, -1):
            half = slice(0, 2) if step == 1 else slice(2, RING)
            piece = self.piece(k, dz, 0, -step if start else 2, half)
            copy = self.copy(k, piece, v, step, 17 + 4 * (dz % RING) + (1 - step) // 2)
            copy.start() if start else copy.wait_recv()

    def send_u(self, k, dz):
        self.along_u(k, dz, True)
        if dz % RING in self.direct:
            self.past_u(k, dz, True)

    def take_u(self, k, dz):
        self.along_u(k, dz, False)
        if dz % RING not in self.direct:
            self.past_u(k, dz, True)

    def send_v(self, k, dz):
        self.past_u(k, dz, False)
        self.along_v(k, dz, True)
        if dz % RING in self.over:
            self.past_v(k, dz, True)

    def take_v(self, k, dz):
        self.along_v(k, dz, False)
        if dz % RING not in self.over:
            self.past_v(k, dz, True)

    def begin(self, parts):
        for k in parts:
            self.along_a(k, True)
        for k in parts:
            self.send_u(k, 0)
        for k in parts:
            if self.far:
                self.past_a(k, True)

    def finish(self, parts):
        def each(step, *planes):
            for dz in planes:
                for k in parts:
                    step(k, dz)

        each(self.take_u, 0)
        each(self.send_v, 0)
        for k in parts:
            self.along_a(k, False)
            if not self.far:
                self.past_a(k, True)
        each(self.send_u, -1, 1)
        each(self.take_u, -1, 1)
        each(self.take_v, 0)
        for k in parts:
            self.past_a(k, False)
        each(self.send_u, 2)
        each(self.send_v, -1, 1)
        each(self.take_u, 2)
        each(self.send_v, 2)
        each(self.take_v, -1, 1, 2)
        each(lambda k, dz: self.past_v(k, dz, False), 0, -1, 1, 2)

    def drain(self):
        for k in range(len(self.parts)):
            ref, first, columns = self.parts[k][:3]
            columns = pl.ds(first, columns)
            sent = (
                ref.at[0, 0, 0:3, :, columns],
                ref.at[0, 0:3, :, :, columns],
                ref.at[0:3, :, :, :, columns],
            )
            for piece, slot in zip(sent, (0, 3, 15)):
                self.copy(k, piece, "x", 1, slot).wait_send()


class Exchange:
    def __init__(self, place, axis, out, into, send, recv):
        self.place, self.axis, self.out, self.into = place, axis, out, into
        self.send, self.recv = send, recv
        self.mine = {"x": place.x, "y": place.y, "z": place.z}[axis]

    def copies(self):
        for step in (1, 3, 2):
            there = self.place.on(self.axis, step)
            source = self.out(there)
            yield there, step, pltpu.make_async_remote_copy(
                src_ref=source,
                dst_ref=self.into.at[self.mine],
                send_sem=self.send.at[step - 1],
                recv_sem=self.recv.at[step - 1],
                device_id={"replica": self.place.at(self.axis, step)},
                device_id_type=MESH,
            )

    def start(self):
        for there, step, copy in self.copies():
            copy.start()

    def wait(self):
        for there, step, copy in self.copies():
            copy.wait_recv()
        for there, step, copy in self.copies():
            copy.wait_send()


def lower_lanes(shape):
    return lax.broadcasted_iota(jnp.int32, shape, len(shape) - 1) < HEAD


def both_halves(block, half):
    low = lower_lanes(block.shape)
    wide = block.astype(F32)
    own = jnp.where(low, wide, 0.0) if half == 0 else jnp.where(low, 0.0, wide)
    return (own + pltpu.roll(own, HEAD, 1)).astype(BF)


def head_rows(ref, group):
    blocks = []
    for j in range(4):
        start = (2 * group + j // 2) * 128
        block = ref[:, start : start + 128]
        low = lower_lanes(block.shape)
        zero = jnp.zeros_like(block)
        blocks.append(jnp.where(low, block, zero) if j % 2 == 0 else jnp.where(low, zero, block))
    return jnp.concatenate(blocks, axis=0)


def put_heads(ref, group, rows):
    low = lower_lanes((TOKENS, 128))
    for b in range(2):
        first = rows[2 * b * TOKENS : (2 * b + 1) * TOKENS]
        second = rows[(2 * b + 1) * TOKENS : (2 * b + 2) * TOKENS]
        start = (2 * group + b) * 128
        ref[:, start : start + 128] = jnp.where(low, first, second).astype(BF)


def kernel(
    emb_in,
    cot_in,
    plan,
    docs,
    gain,
    wq_share,
    wo_share,
    stash_in,
    now_in,
    adam_m,
    adam_v,
    stash_out,
    next_out,
    m_out,
    v_out,
    emb,
    cot,
    kv_stash,
    kv_now,
    tags,
    wq,
    wo,
    wq_t,
    wo_t,
    stash_t,
    now_t,
    hid,
    up,
    fwd_out,
    bwd_out,
    wide,
    scale,
    q,
    kv,
    probs,
    mixed,
    mixed_grad,
    dq,
    kg,
    n_t,
    n_y,
    n_x,
    k_y,
    k_x,
    x_buf,
    x_all,
    y_buf,
    y_all,
    z_buf,
    z_all,
    w_send,
    w_recv,
    o_send,
    o_recv,
    hop_send,
    hop_recv,
    trade_send,
    trade_recv,
    load_sem,
):
    place = Place()
    section = lax.axis_index("section")
    last = RING - 1

    loads = [
        pltpu.make_async_copy(src, dst, load_sem.at[i])
        for i, (src, dst) in enumerate(
            ((emb_in, emb), (cot_in, cot), (stash_in, kv_stash), (now_in, kv_now))
        )
    ]
    for load in loads:
        load.start()

    def load_wait():
        for load in loads:
            load.wait()

    barrier = pltpu.get_barrier_semaphore()
    for axis in ("x", "y", "z"):
        for step in (1, 2, 3):
            pl.semaphore_signal(
                barrier, inc=1, device_id={"replica": place.at(axis, step)}, device_id_type=MESH
            )
    for step in (1, -1):
        pl.semaphore_signal(
            barrier, inc=1, device_id={"section": wrap(section + step)}, device_id_type=MESH
        )
    pl.semaphore_wait(barrier, 11)

    def columns(c, size=WIDE):
        return slice(c * size, (c + 1) * size)

    def hop(way, src, dst, c, to):
        return pltpu.make_async_remote_copy(
            src_ref=src.at[:, columns(c)],
            dst_ref=dst.at[:, columns(c)],
            send_sem=hop_send.at[way, c],
            recv_sem=hop_recv.at[way, c],
            device_id={"section": wrap(section + to)},
            device_id_type=MESH,
        )

    def drain_hops():
        @pl.when(section < last)
        def _():
            for c in range(CHUNKS):
                hop(0, fwd_out, hid, c, 1).wait_send()

        @pl.when(section > 0)
        def _():
            for c in range(CHUNKS):
                hop(1, bwd_out, up, c, -1).wait_send()

    def four(block):
        return block[:, :128] + block[:, 128:256] + block[:, 256:384] + block[:, 384:]

    def allowed():
        tag = jnp.broadcast_to(tags[:1, :], (TOKENS, TOKENS))
        row = lax.broadcasted_iota(jnp.int32, (TOKENS, TOKENS), 0)
        col = lax.broadcasted_iota(jnp.int32, (TOKENS, TOKENS), 1)
        return (tag == tag.T) & (row // 32 == col // 32) & (row <= col)

    def project():
        @pl.when(section == 0)
        def _():
            for i in range(RING):
                hid[i * 32 : (i + 1) * 32, :] = emb[0, plan[0, i]]

        for c in range(CHUNKS):
            cols = columns(c)

            @pl.when(section > 0)
            def _():
                hop(0, fwd_out, hid, c, -1).wait_recv()

            own = hid[:, cols].astype(F32)
            gained = (own * gain[:, cols].astype(F32)).astype(BF)
            squares = four(own * own)
            products = (
                mm(gained, wq[c].reshape(WIDE, QW)),
                mm(gained[:HALF], kv_stash[0, cols, :]),
                mm(gained[HALF:], kv_now[0, cols, :]),
            )
            if c == 0:
                wide[:, :QW] = products[0]
                wide[:HALF, QW : QW + KVW] = products[1]
                wide[HALF:, QW : QW + KVW] = products[2]
                scale[...] = squares
            else:
                wide[:, :QW] += products[0]
                wide[:HALF, QW : QW + KVW] += products[1]
                wide[HALF:, QW : QW + KVW] += products[2]
                scale[...] += squares
        mean = jnp.sum(scale[...], axis=-1, keepdims=True) * (1.0 / WIDTH)
        r = lax.rsqrt(mean + norm_eps)
        scale[...] = jnp.broadcast_to(r, (TOKENS, 128))
        q[...] = (wide[:, :QW] * r).astype(BF)
        kv[...] = (wide[:, QW : QW + KVW] * r).astype(BF)

        mask = jnp.concatenate([allowed()] * 4, axis=1)
        for group in range(4):
            start = (group // 2) * 128
            keys = both_halves(kv[:, start : start + 128], group % 2)
            values = both_halves(kv[:, 256 + start : 256 + start + 128], group % 2)
            score = mm(keys, head_rows(q, group), NT)
            weight = jnp.where(mask, jnp.exp(score * (HEAD**-0.5)), 0.0)
            prob = weight / jnp.sum(weight, axis=0, keepdims=True)
            probs[group] = prob

            @pl.when(section < last)
            def _():
                put_heads(mixed, group, mm(prob.astype(BF), values, TN))

    def prepare():
        def turn(i, carry):
            rows = pl.ds(pl.multiple_of(i * WIDE, WIDE), WIDE)
            wq_t[:, rows] = wq[i].reshape(WIDE, QW).T
            stash_t[:, rows] = kv_stash[0, rows, :].T
            now_t[:, rows] = kv_now[0, rows, :].T
            return carry

        def turn_out(i, carry):
            rows = pl.ds(pl.multiple_of(i * 256, 256), 256)
            wo_t[:, rows] = wo[i].reshape(256, WIDTH).T
            return carry

        lax.fori_loop(0, RING, turn_out, 0)
        lax.fori_loop(0, RING, turn, 0)

    def trade(index, axis, out, into):
        return Exchange(place, axis, out, into, trade_send.at[index], trade_recv.at[index])

    n_trades = (
        trade(0, "y", lambda there: n_t.at[0:2, there], n_y),
        trade(1, "x", lambda there: n_t.at[2:4, :, there], n_x),
    )
    k_trades = (trade(2, "y", lambda there: kg, k_y), trade(3, "x", lambda there: kg, k_x))

    def share_normed():
        for block in range(RING * RING):
            cols = columns(block, 128)
            own = hid[:, cols].astype(F32) * scale[...] * gain[:, cols].astype(F32)
            n_t[block // RING, block % RING] = own.astype(BF).T.reshape(RING, 32, TOKENS)
        n_y[place.y] = n_t[0:2, place.y]
        n_x[place.x] = n_t[2:4, :, place.x]
        for one in n_trades:
            one.start()

    def make_mixed_grad(streamed):
        for c in range(CHUNKS):
            if streamed:
                hop(1, bwd_out, up, c, 1).wait_recv()
            part = mm(up[:, columns(c)], wo_t[columns(c), :])
            if c == 0:
                wide[:, :QW] = part
            elif c < CHUNKS - 1:
                wide[:, :QW] += part
            else:
                mixed_grad[...] = (wide[:, :QW] + part).astype(BF)

    weights = Gather(
        place,
        [
            (wq, 0, 384, "z", "x", "y"),
            (wq, 384, 384, "z", "y", "x"),
            (wq, 768, 256, "x", "y", "z"),
            (wo, 0, 896, "z", "x", "y"),
            (wo, 896, 896, "z", "y", "x"),
            (wo, 1792, 256, "y", "x", "z"),
        ],
        w_send,
        w_recv,
        (0,),
        False,
        (),
    )
    wq[place.z, place.y, place.x] = wq_share[0]
    wo[place.z, place.y, place.x] = wo_share[0]

    weights.begin(range(6))
    for i in range(RING):
        tags[:1, i * 32 : (i + 1) * 32] = docs[0, pl.ds(plan[0, i], 1), :].astype(F32)
    weights.finish(range(6))

    load_wait()

    @pl.when(section == last)
    def _():
        prepare()
        for i in range(RING):
            up[i * 32 : (i + 1) * 32, :] = cot[0, plan[0, i]]
        make_mixed_grad(False)

    project()

    @pl.when(section < last)
    def _():
        for c in range(CHUNKS):
            cols = columns(c)
            fwd_out[:, cols] = (hid[:, cols].astype(F32) + mm(mixed[...], wo[:, :, :, :, cols].reshape(QW, WIDE))).astype(BF)
            hop(0, fwd_out, hid, c, 1).start()
        prepare()
        share_normed()
        make_mixed_grad(True)

    low = lower_lanes((TOKENS, 128))
    folded = []
    for group in range(4):
        start = (group // 2) * 128
        keys = both_halves(kv[:, start : start + 128], group % 2)
        values = both_halves(kv[:, 256 + start : 256 + start + 128], group % 2)
        heads = head_rows(q, group)
        heads_grad = head_rows(mixed_grad, group)
        prob = probs[group]
        prob_grad = mm(values, heads_grad, NT)
        inner = jnp.sum(prob_grad * prob, axis=0, keepdims=True)
        score_grad = (prob * (prob_grad - inner) * (HEAD**-0.5)).astype(BF)
        put_heads(dq, group, mm(score_grad, keys, TN))
        dk = mm(score_grad, heads)
        dv = mm(prob.astype(BF), heads_grad)
        folded.append((dk + pltpu.roll(dk, HEAD, 1), dv + pltpu.roll(dv, HEAD, 1)))
        if group % 2 == 1:
            for part in range(2):
                both = jnp.where(low, folded[group - 1][part], folded[group][part]).astype(BF)
                kg[:, part * 256 + start : part * 256 + start + 128] = both

    k_y[place.y] = kg[...]
    k_x[place.x] = kg[...]
    for one in k_trades:
        one.start()

    @pl.when(section > 0)
    def _():
        total = jnp.zeros((TOKENS, 128), F32)
        for c in range(CHUNKS):
            cols = columns(c)
            first = mm(kg[:HALF, :], stash_t[:, cols])
            second = mm(kg[HALF:, :], now_t[:, cols])
            part = mm(dq[...], wq_t[:, cols]) + jnp.concatenate([first, second], axis=0)
            part = part * gain[:, cols].astype(F32)
            wide[:, cols] = part
            total = total + four(part * hid[:, cols].astype(F32))
        r = scale[...]
        inner = jnp.sum(total, axis=-1, keepdims=True) * (1.0 / WIDTH)
        inner = jnp.broadcast_to(inner, (TOKENS, 128)) * (r * r * r)
        for c in range(CHUNKS):
            for d in range(RING):
                cols = columns(c * RING + d, 128)
                through = wide[:, cols] * r - hid[:, cols].astype(F32) * inner
                bwd_out[:, cols] = (up[:, cols].astype(F32) + through).astype(BF)
            hop(1, bwd_out, up, c, -1).start()

    @pl.when(section == last)
    def _():
        share_normed()

    for one in n_trades + k_trades:
        one.wait()
    token = lax.broadcasted_iota(jnp.int32, (256, RING * TOKENS), 1)
    early = lax.rem(token, TOKENS) < HALF
    for n_all, k_all, buf in ((n_y, k_y, x_buf), (n_x, k_x, y_buf)):
        left = jnp.concatenate([n_all[src].reshape(256, TOKENS) for src in range(RING)], axis=1)
        right = k_all[...].reshape(RING * TOKENS, KVW)
        zero = jnp.zeros_like(left)
        for step in range(2):
            own = jnp.where(early, left, zero) if step == 0 else jnp.where(early, zero, left)
            part = mm(own, right).astype(BF).reshape(2, RING, 32, KVW)
            for there in range(RING):
                buf[there, :, :, step * KVW : (step + 1) * KVW] = part[:, there]
        one = (
            trade(4, "x", lambda there: x_buf.at[there], x_all)
            if buf is x_buf
            else trade(5, "y", lambda there: y_buf.at[there], y_all)
        )
        one.start()
    x_all[place.x] = x_buf[place.x]
    y_all[place.y] = y_buf[place.y]
    trade(4, "x", lambda there: x_buf.at[there], x_all).wait()
    trade(5, "y", lambda there: y_buf.at[there], y_all).wait()
    for start, parts in ((0, x_all), (2, y_all)):
        total = parts[0].astype(F32)
        for src in range(1, RING):
            total = total + parts[src].astype(F32)
        z_buf[start : start + 2] = total.astype(BF)
    z_trade = trade(6, "z", lambda there: z_buf.at[there], z_all)
    z_all[place.z] = z_buf[place.z]
    z_trade.start()
    z_trade.wait()
    grads = z_all[0].astype(F32)
    for src in range(1, RING):
        grads = grads + z_all[src].astype(F32)
    grads = grads * (1.0 / REPLICAS)
    outputs = Gather(
        place,
        [
            (stash_out, 0, 384, "z", "x", "y"),
            (next_out, 0, 384, "z", "y", "x"),
            (stash_out, 384, 128, "x", "y", "z"),
            (next_out, 384, 128, "y", "x", "z"),
        ],
        o_send,
        o_recv,
        (0, 1, 2, 3),
        True,
        (2,),
    )
    own = pl.ds(pl.multiple_of(place.me * 32, 32), 32)
    rows = kv_now[0, own, :]
    first, second = adam_m[0], adam_v[0]
    for step, target in ((0, stash_out), (1, next_out)):
        grad = grads[:, step * KVW : (step + 1) * KVW]
        first_new = beta_first * first.astype(F32) + (1.0 - beta_first) * grad
        second_new = beta_second * second.astype(F32) + (1.0 - beta_second) * grad * grad
        moved = rows.astype(F32) - learn_rate * first_new / (jnp.sqrt(second_new) + adam_eps)
        rows, first, second = moved.astype(BF), first_new.astype(BF), second_new.astype(BF)
        target[place.z, place.y, place.x] = rows
        outputs.begin((step, step + 2))
    m_out[0] = first
    v_out[0] = second
    outputs.finish(range(4))

    weights.drain()
    outputs.drain()
    drain_hops()


def place_results(*refs):
    sem = refs[12]
    loads, stores = [], []
    for i in range(4):
        for part in range(RING if i < 2 else 1):
            slot = len(loads)
            src, dst, held = (refs[j + i].at[part] for j in (0, 4, 8))
            loads.append(pltpu.make_async_copy(src, held, sem.at[0, slot]))
            stores.append(pltpu.make_async_copy(held, dst, sem.at[1, slot]))
    for load in loads:
        load.start()
    for load, store in zip(loads, stores):
        load.wait()
        store.start()
    for store in stores:
        store.wait()


def body(
    embeddings, cotangent, plan, doc_ids, norm_gain, w_query, w_out, kv_stash, kv_now, adam_m, adam_v
):
    vmem = pl.BlockSpec(memory_space=pltpu.VMEM)
    smem = pl.BlockSpec(memory_space=pltpu.SMEM)
    hbm = pl.BlockSpec(memory_space=pl.ANY)
    dma = pltpu.SemaphoreType.DMA
    version = jax.ShapeDtypeStruct((RING, RING, RING, 32, KVW), BF)
    moment = jax.ShapeDtypeStruct((1, 32, KVW), BF)
    results = pl.pallas_call(
        kernel,
        out_shape=(version, version, moment, moment),
        in_specs=[hbm, hbm, smem, vmem, vmem, vmem, vmem, hbm, hbm, vmem, vmem],
        out_specs=(vmem,) * 4,
        scratch_shapes=[
            pltpu.VMEM((1, 4, 32, WIDTH), BF),
            pltpu.VMEM((1, 4, 32, WIDTH), BF),
            pltpu.VMEM((1, WIDTH, KVW), BF),
            pltpu.VMEM((1, WIDTH, KVW), BF),
            pltpu.VMEM((8, TOKENS), F32),
            pltpu.VMEM((RING, RING, RING, 32, QW), BF),
            pltpu.VMEM((RING, RING, RING, 16, WIDTH), BF),
            pltpu.VMEM((QW, WIDTH), BF),
            pltpu.VMEM((WIDTH, QW), BF),
            pltpu.VMEM((KVW, WIDTH), BF),
            pltpu.VMEM((KVW, WIDTH), BF),
            pltpu.VMEM((TOKENS, WIDTH), BF),
            pltpu.VMEM((TOKENS, WIDTH), BF),
            pltpu.VMEM((TOKENS, WIDTH), BF),
            pltpu.VMEM((TOKENS, WIDTH), BF),
            pltpu.VMEM((TOKENS, WIDTH), F32),
            pltpu.VMEM((TOKENS, 128), F32),
            pltpu.VMEM((TOKENS, QW), BF),
            pltpu.VMEM((TOKENS, KVW), BF),
            pltpu.VMEM((4, TOKENS, 4 * TOKENS), F32),
            pltpu.VMEM((TOKENS, QW), BF),
            pltpu.VMEM((TOKENS, QW), BF),
            pltpu.VMEM((TOKENS, QW), BF),
            pltpu.VMEM((TOKENS, KVW), BF),
            pltpu.VMEM((RING, RING, RING, 32, TOKENS), BF),
            pltpu.VMEM((RING, 2, RING, 32, TOKENS), BF),
            pltpu.VMEM((RING, 2, RING, 32, TOKENS), BF),
            pltpu.VMEM((RING, TOKENS, KVW), BF),
            pltpu.VMEM((RING, TOKENS, KVW), BF),
            pltpu.VMEM((RING, 2, 32, 2 * KVW), BF),
            pltpu.VMEM((RING, 2, 32, 2 * KVW), BF),
            pltpu.VMEM((RING, 2, 32, 2 * KVW), BF),
            pltpu.VMEM((RING, 2, 32, 2 * KVW), BF),
            pltpu.VMEM((RING, 32, 2 * KVW), BF),
            pltpu.VMEM((RING, 32, 2 * KVW), BF),
            dma((6, 3)),
            dma((6, 31)),
            dma((4, 3)),
            dma((4, 31)),
            dma((2, CHUNKS)),
            dma((2, CHUNKS)),
            dma((7, RING - 1)),
            dma((7, RING - 1)),
            dma((4,)),
        ],
        compiler_params=pltpu.CompilerParams(
            collective_id=0, has_side_effects=True, vmem_limit_bytes=56 * 1024 * 1024
        ),
    )(embeddings, cotangent, plan, doc_ids, norm_gain, w_query, w_out, kv_stash, kv_now, adam_m, adam_v)
    pieces = 2 * RING + 2
    stash, current, first, second = pl.pallas_call(
        place_results,
        out_shape=[jax.ShapeDtypeStruct(r.shape, BF) for r in results],
        in_specs=[hbm] * 4,
        out_specs=[hbm] * 4,
        scratch_shapes=[pltpu.VMEM(r.shape, BF) for r in results] + [dma((2, pieces))],
        compiler_params=pltpu.CompilerParams(vmem_limit_bytes=60 * 1024 * 1024),
    )(*results)
    shape = (1, WIDTH, KVW)
    return stash.reshape(shape), current.reshape(shape), first, second


def solution(mesh):
    placed = (
        P("replica", None, None, None),
        P("replica", None, None, None),
        P("replica", None),
        P("replica", None, None),
        P("section", None),
        P("section", "replica", None),
        P("section", "replica", None),
        P("section", None, None),
        P("section", None, None),
        P("section", "replica", None),
        P("section", "replica", None),
    )
    return jax.shard_map(
        body,
        mesh=mesh,
        in_specs=placed,
        out_specs=(
            P("section", None, None),
            P("section", None, None),
            P("section", "replica", None),
            P("section", "replica", None),
        ),
        check_vma=False,
    )
```

```python
import functools

import jax
import jax.numpy as jnp
from jax import lax
from jax.experimental import pallas as pl
from jax.experimental.pallas import tpu as pltpu
from jax.sharding import PartitionSpec as P

HEAD = 64
RING = 4
REPLICAS = 64
TOKENS = 128
HALF = 64
WIDTH = 2048
QW = 1024
KVW = 512
WIDE = 512
CHUNKS = 4
BF = jnp.bfloat16
F32 = jnp.float32
MESH = pl.DeviceIdType.MESH

beta_first = 0.9
beta_second = 0.999
learn_rate = 0.003
adam_eps = 1e-08
norm_eps = 1e-05

NN = (((1,), (0,)), ((), ()))
NT = (((1,), (1,)), ((), ()))
TN = (((0,), (0,)), ((), ()))


def mm(a, b, dims=NN):
    return lax.dot_general(a, b, dims, preferred_element_type=F32)


def wrap(v):
    return lax.rem(v + RING, RING)


class Place:
    def __init__(self):
        me = lax.axis_index("replica")
        self.me = me
        self.z = me // 16
        self.y = lax.rem(me // 4, RING)
        self.x = lax.rem(me, RING)
        self.line = {}
        for axis, own in (("z", self.z), ("y", self.y), ("x", self.x)):
            self.line[axis] = [own] + [wrap(own + step) for step in range(1, RING)]

    def on(self, axis, step):
        return self.line[axis][step % RING]

    def at(self, axis, step):
        spot = {"z": self.z, "y": self.y, "x": self.x}
        spot[axis] = self.on(axis, step)
        return (spot["z"] * RING + spot["y"]) * RING + spot["x"]


class Gather:
    def __init__(self, place, parts, send, recv, direct, far, over):
        self.place, self.parts, self.send, self.recv = place, parts, send, recv
        self.direct, self.far, self.over = direct, far, over
        self.peer = {
            (axis, step): place.at(axis, step) for axis in ("x", "y", "z") for step in (1, -1, 2)
        }

    def piece(self, k, da, du=0, dv=0, many=None):
        ref, first, columns, a, u, v = self.parts[k]
        spot = {a: self.place.on(a, da), u: self.place.on(u, du), v: self.place.on(v, dv)}
        if many is not None:
            spot[u] = many
        return ref.at[spot["z"], spot["y"], spot["x"], :, pl.ds(first, columns)]

    def copy(self, k, piece, axis, step, slot):
        stage = 0 if slot < 3 else 1 if slot < 15 else 2
        return pltpu.make_async_remote_copy(
            src_ref=piece,
            dst_ref=piece,
            send_sem=self.send.at[k, stage],
            recv_sem=self.recv.at[k, slot],
            device_id={"replica": self.peer[axis, step]},
            device_id_type=MESH,
        )

    def along_a(self, k, start):
        a = self.parts[k][3]
        for step in (1, -1):
            copy = self.copy(k, self.piece(k, 0 if start else -step), a, step, (1 - step) // 2)
            copy.start() if start else copy.wait_recv()

    def past_a(self, k, start):
        a = self.parts[k][3]
        step = 1 if k % 2 else -1
        source = -step
        if self.far:
            step, source = 2, 0
        copy = self.copy(k, self.piece(k, source if start else 2), a, step, 2)
        copy.start() if start else copy.wait_recv()

    def along_u(self, k, dz, start):
        u = self.parts[k][4]
        for step in (1, -1):
            piece = self.piece(k, dz, 0 if start else -step)
            copy = self.copy(k, piece, u, step, 3 + 3 * (dz % RING) + (1 - step) // 2)
            copy.start() if start else copy.wait_recv()

    def past_u(self, k, dz, start):
        u = self.parts[k][4]
        step = 1 if dz % 2 else -1
        source = -step
        if dz % RING in self.direct:
            step, source = 2, 0
        piece = self.piece(k, dz, source if start else 2)
        copy = self.copy(k, piece, u, step, 3 + 3 * (dz % RING) + 2)
        copy.start() if start else copy.wait_recv()

    def along_v(self, k, dz, start):
        v = self.parts[k][5]
        for step in (1, -1):
            piece = self.piece(k, dz, 0, 0 if start else -step, slice(0, RING))
            copy = self.copy(k, piece, v, step, 15 + 4 * (dz % RING) + (1 - step) // 2)
            copy.start() if start else copy.wait_recv()

    def past_v(self, k, dz, start):
        v = self.parts[k][5]
        if dz % RING in self.over:
            piece = self.piece(k, dz, 0, 0 if start else 2, slice(0, RING))
            copy = self.copy(k, piece, v, 2, 17 + 4 * (dz % RING))
            copy.start() if start else copy.wait_recv()
            return
        for step in (1, -1):
            half = slice(0, 2) if step == 1 else slice(2, RING)
            piece = self.piece(k, dz, 0, -step if start else 2, half)
            copy = self.copy(k, piece, v, step, 17 + 4 * (dz % RING) + (1 - step) // 2)
            copy.start() if start else copy.wait_recv()

    def send_u(self, k, dz):
        self.along_u(k, dz, True)
        if dz % RING in self.direct:
            self.past_u(k, dz, True)

    def take_u(self, k, dz):
        self.along_u(k, dz, False)
        if dz % RING not in self.direct:
            self.past_u(k, dz, True)

    def send_v(self, k, dz):
        self.past_u(k, dz, False)
        self.along_v(k, dz, True)
        if dz % RING in self.over:
            self.past_v(k, dz, True)

    def take_v(self, k, dz):
        self.along_v(k, dz, False)
        if dz % RING not in self.over:
            self.past_v(k, dz, True)

    def begin(self, parts):
        for k in parts:
            self.along_a(k, True)
        for k in parts:
            self.send_u(k, 0)
        for k in parts:
            if self.far:
                self.past_a(k, True)

    def finish(self, parts):
        def each(step, *planes):
            for dz in planes:
                for k in parts:
                    step(k, dz)

        each(self.take_u, 0)
        each(self.send_v, 0)
        for k in parts:
            self.along_a(k, False)
            if not self.far:
                self.past_a(k, True)
        each(self.send_u, -1, 1)
        if not self.far:
            each(self.take_u, -1, 1)
            each(self.take_v, 0)
        for k in parts:
            self.past_a(k, False)
        each(self.send_u, 2)
        if self.far:
            each(self.take_u, -1, 1)
        each(self.send_v, -1, 1)
        each(self.take_u, 2)
        each(self.send_v, 2)
        if self.far:
            each(self.take_v, 0)
        each(self.take_v, -1, 1, 2)
        each(lambda k, dz: self.past_v(k, dz, False), 0, -1, 1, 2)

    def drain(self):
        for k in range(len(self.parts)):
            ref, first, columns = self.parts[k][:3]
            columns = pl.ds(first, columns)
            sent = (
                ref.at[0, 0, 0:3, :, columns],
                ref.at[0, 0:3, :, :, columns],
                ref.at[0:3, :, :, :, columns],
            )
            for piece, slot in zip(sent, (0, 3, 15)):
                self.copy(k, piece, "x", 1, slot).wait_send()


class Exchange:
    def __init__(self, place, axis, out, into, send, recv):
        self.place, self.axis, self.out, self.into = place, axis, out, into
        self.send, self.recv = send, recv
        self.mine = {"x": place.x, "y": place.y, "z": place.z}[axis]

    def copies(self):
        for step in (1, 3, 2):
            there = self.place.on(self.axis, step)
            source = self.out(there)
            yield there, step, pltpu.make_async_remote_copy(
                src_ref=source,
                dst_ref=self.into.at[self.mine],
                send_sem=self.send.at[step - 1],
                recv_sem=self.recv.at[step - 1],
                device_id={"replica": self.place.at(self.axis, step)},
                device_id_type=MESH,
            )

    def start(self):
        for there, step, copy in self.copies():
            copy.start()

    def wait(self):
        for there, step, copy in self.copies():
            copy.wait_recv()
        for there, step, copy in self.copies():
            copy.wait_send()


def lower_lanes(shape):
    return lax.broadcasted_iota(jnp.int32, shape, len(shape) - 1) < HEAD


def both_halves(block, half):
    low = lower_lanes(block.shape)
    wide = block.astype(F32)
    own = jnp.where(low, wide, 0.0) if half == 0 else jnp.where(low, 0.0, wide)
    return (own + pltpu.roll(own, HEAD, 1)).astype(BF)


def head_rows(ref, group):
    blocks = []
    for j in range(4):
        start = (2 * group + j // 2) * 128
        block = ref[:, start : start + 128]
        low = lower_lanes(block.shape)
        zero = jnp.zeros_like(block)
        blocks.append(jnp.where(low, block, zero) if j % 2 == 0 else jnp.where(low, zero, block))
    return jnp.concatenate(blocks, axis=0)


def put_heads(ref, group, rows):
    low = lower_lanes((TOKENS, 128))
    for b in range(2):
        first = rows[2 * b * TOKENS : (2 * b + 1) * TOKENS]
        second = rows[(2 * b + 1) * TOKENS : (2 * b + 2) * TOKENS]
        start = (2 * group + b) * 128
        ref[:, start : start + 128] = jnp.where(low, first, second).astype(BF)


def kernel(
    emb_in,
    cot_in,
    plan,
    docs,
    gain,
    wq_share,
    wo_share,
    stash_in,
    now_in,
    adam_m,
    adam_v,
    stash_out,
    next_out,
    m_out,
    v_out,
    emb,
    cot,
    kv_stash,
    kv_now,
    tags,
    wq,
    wo,
    wq_t,
    wo_t,
    stash_t,
    now_t,
    hid,
    up,
    fwd_out,
    bwd_out,
    wide,
    scale,
    q,
    kv,
    probs,
    mixed,
    mixed_grad,
    dq,
    kg,
    n_t,
    n_y,
    n_x,
    k_y,
    k_x,
    lefts,
    x_buf,
    x_all,
    y_buf,
    y_all,
    z_buf,
    z_all,
    w_send,
    w_recv,
    o_send,
    o_recv,
    hop_send,
    hop_recv,
    trade_send,
    trade_recv,
    load_sem,
):
    place = Place()
    section = lax.axis_index("section")
    last = RING - 1

    loads = [
        pltpu.make_async_copy(src, dst, load_sem.at[i])
        for i, (src, dst) in enumerate(
            ((emb_in, emb), (cot_in, cot), (stash_in, kv_stash), (now_in, kv_now))
        )
    ]
    for load in loads:
        load.start()

    def load_wait():
        for load in loads:
            load.wait()

    barrier = pltpu.get_barrier_semaphore()
    for axis in ("x", "y", "z"):
        for step in (1, 2, 3):
            pl.semaphore_signal(
                barrier, inc=1, device_id={"replica": place.at(axis, step)}, device_id_type=MESH
            )
    for step in (1, -1):
        pl.semaphore_signal(
            barrier, inc=1, device_id={"section": wrap(section + step)}, device_id_type=MESH
        )
    pl.semaphore_wait(barrier, 11)

    def columns(c, size=WIDE):
        return slice(c * size, (c + 1) * size)

    def hop(way, src, dst, c, to):
        return pltpu.make_async_remote_copy(
            src_ref=src.at[:, columns(c)],
            dst_ref=dst.at[:, columns(c)],
            send_sem=hop_send.at[way, c],
            recv_sem=hop_recv.at[way, c],
            device_id={"section": wrap(section + to)},
            device_id_type=MESH,
        )

    def drain_hops():
        @pl.when(section < last)
        def _():
            for c in range(CHUNKS):
                hop(0, fwd_out, hid, c, 1).wait_send()

        @pl.when(section > 0)
        def _():
            for c in range(CHUNKS):
                hop(1, bwd_out, up, c, -1).wait_send()

    def four(block):
        return block[:, :128] + block[:, 128:256] + block[:, 256:384] + block[:, 384:]

    def allowed():
        tag = jnp.broadcast_to(tags[:1, :], (TOKENS, TOKENS))
        row = lax.broadcasted_iota(jnp.int32, (TOKENS, TOKENS), 0)
        col = lax.broadcasted_iota(jnp.int32, (TOKENS, TOKENS), 1)
        return (tag == tag.T) & (row // 32 == col // 32) & (row <= col)

    def project():
        @pl.when(section == 0)
        def _():
            for i in range(RING):
                hid[i * 32 : (i + 1) * 32, :] = emb[0, plan[0, i]]

        for c in range(CHUNKS):
            cols = columns(c)

            @pl.when(section > 0)
            def _():
                hop(0, fwd_out, hid, c, -1).wait_recv()

            own = hid[:, cols].astype(F32)
            gained = (own * gain[:, cols].astype(F32)).astype(BF)
            squares = four(own * own)
            products = (
                mm(gained, wq[c].reshape(WIDE, QW)),
                mm(gained[:HALF], kv_stash[0, cols, :]),
                mm(gained[HALF:], kv_now[0, cols, :]),
            )
            if c == 0:
                wide[:, :QW] = products[0]
                wide[:HALF, QW : QW + KVW] = products[1]
                wide[HALF:, QW : QW + KVW] = products[2]
                scale[...] = squares
            else:
                wide[:, :QW] += products[0]
                wide[:HALF, QW : QW + KVW] += products[1]
                wide[HALF:, QW : QW + KVW] += products[2]
                scale[...] += squares
        mean = jnp.sum(scale[...], axis=-1, keepdims=True) * (1.0 / WIDTH)
        r = lax.rsqrt(mean + norm_eps)
        scale[...] = jnp.broadcast_to(r, (TOKENS, 128))
        q[...] = (wide[:, :QW] * r).astype(BF)
        kv[...] = (wide[:, QW : QW + KVW] * r).astype(BF)

        mask = jnp.concatenate([allowed()] * 4, axis=1)
        for group in range(4):
            start = (group // 2) * 128
            keys = both_halves(kv[:, start : start + 128], group % 2)
            values = both_halves(kv[:, 256 + start : 256 + start + 128], group % 2)
            score = mm(keys, head_rows(q, group), NT)
            weight = jnp.where(mask, jnp.exp(score * (HEAD**-0.5)), 0.0)
            prob = weight / jnp.sum(weight, axis=0, keepdims=True)
            probs[group] = prob

            @pl.when(section < last)
            def _():
                put_heads(mixed, group, mm(prob.astype(BF), values, TN))

    def prepare():
        def turn(i, carry):
            rows = pl.ds(pl.multiple_of(i * WIDE, WIDE), WIDE)
            wq_t[:, rows] = wq[i].reshape(WIDE, QW).T
            stash_t[:, rows] = kv_stash[0, rows, :].T
            now_t[:, rows] = kv_now[0, rows, :].T
            return carry

        def turn_out(i, carry):
            rows = pl.ds(pl.multiple_of(i * 256, 256), 256)
            wo_t[:, rows] = wo[i].reshape(256, WIDTH).T
            return carry

        lax.fori_loop(0, RING, turn_out, 0)
        lax.fori_loop(0, RING, turn, 0)

    def trade(index, axis, out, into):
        return Exchange(place, axis, out, into, trade_send.at[index], trade_recv.at[index])

    n_trades = (
        trade(0, "y", lambda there: n_t.at[0:2, there], n_y),
        trade(1, "x", lambda there: n_t.at[2:4, :, there], n_x),
    )
    k_trades = (trade(2, "y", lambda there: kg, k_y), trade(3, "x", lambda there: kg, k_x))

    def share_normed():
        for block in range(RING * RING):
            cols = columns(block, 128)
            own = hid[:, cols].astype(F32) * scale[...] * gain[:, cols].astype(F32)
            n_t[block // RING, block % RING] = own.astype(BF).T.reshape(RING, 32, TOKENS)
        n_y[place.y] = n_t[0:2, place.y]
        n_x[place.x] = n_t[2:4, :, place.x]
        for one in n_trades:
            one.start()

    def make_mixed_grad(streamed):
        for c in range(CHUNKS):
            if streamed:
                hop(1, bwd_out, up, c, 1).wait_recv()
            part = mm(up[:, columns(c)], wo_t[columns(c), :])
            if c == 0:
                wide[:, :QW] = part
            elif c < CHUNKS - 1:
                wide[:, :QW] += part
            else:
                mixed_grad[...] = (wide[:, :QW] + part).astype(BF)

    weights = Gather(
        place,
        [
            (wq, 0, 384, "z", "x", "y"),
            (wq, 384, 384, "z", "y", "x"),
            (wq, 768, 256, "x", "y", "z"),
            (wo, 0, 896, "z", "x", "y"),
            (wo, 896, 896, "z", "y", "x"),
            (wo, 1792, 256, "y", "x", "z"),
        ],
        w_send,
        w_recv,
        (0,),
        False,
        (),
    )
    wq[place.z, place.y, place.x] = wq_share[0]
    wo[place.z, place.y, place.x] = wo_share[0]

    weights.begin(range(6))
    for i in range(RING):
        tags[:1, i * 32 : (i + 1) * 32] = docs[0, pl.ds(plan[0, i], 1), :].astype(F32)
    weights.finish(range(6))

    load_wait()

    @pl.when(section == last)
    def _():
        prepare()
        for i in range(RING):
            up[i * 32 : (i + 1) * 32, :] = cot[0, plan[0, i]]
        make_mixed_grad(False)

    project()

    @pl.when(section < last)
    def _():
        for c in range(CHUNKS):
            cols = columns(c)
            fwd_out[:, cols] = (hid[:, cols].astype(F32) + mm(mixed[...], wo[:, :, :, :, cols].reshape(QW, WIDE))).astype(BF)
            hop(0, fwd_out, hid, c, 1).start()
        prepare()
        share_normed()
        make_mixed_grad(True)

    low = lower_lanes((TOKENS, 128))
    folded = []
    for group in range(4):
        start = (group // 2) * 128
        keys = both_halves(kv[:, start : start + 128], group % 2)
        values = both_halves(kv[:, 256 + start : 256 + start + 128], group % 2)
        heads = head_rows(q, group)
        heads_grad = head_rows(mixed_grad, group)
        prob = probs[group]
        prob_grad = mm(values, heads_grad, NT)
        inner = jnp.sum(prob_grad * prob, axis=0, keepdims=True)
        score_grad = (prob * (prob_grad - inner) * (HEAD**-0.5)).astype(BF)
        put_heads(dq, group, mm(score_grad, keys, TN))
        dk = mm(score_grad, heads)
        dv = mm(prob.astype(BF), heads_grad)
        folded.append((dk + pltpu.roll(dk, HEAD, 1), dv + pltpu.roll(dv, HEAD, 1)))
        if group % 2 == 1:
            for part in range(2):
                both = jnp.where(low, folded[group - 1][part], folded[group][part]).astype(BF)
                kg[:, part * 256 + start : part * 256 + start + 128] = both

    k_y[place.y] = kg[...]
    k_x[place.x] = kg[...]
    for one in k_trades:
        one.start()

    @pl.when(section > 0)
    def _():
        total = jnp.zeros((TOKENS, 128), F32)
        for c in range(CHUNKS):
            cols = columns(c)
            first = mm(kg[:HALF, :], stash_t[:, cols])
            second = mm(kg[HALF:, :], now_t[:, cols])
            part = mm(dq[...], wq_t[:, cols]) + jnp.concatenate([first, second], axis=0)
            part = part * gain[:, cols].astype(F32)
            wide[:, cols] = part
            total = total + four(part * hid[:, cols].astype(F32))
        r = scale[...]
        inner = jnp.sum(total, axis=-1, keepdims=True) * (1.0 / WIDTH)
        inner = jnp.broadcast_to(inner, (TOKENS, 128)) * (r * r * r)
        for c in range(CHUNKS):
            for d in range(RING):
                cols = columns(c * RING + d, 128)
                through = wide[:, cols] * r - hid[:, cols].astype(F32) * inner
                bwd_out[:, cols] = (up[:, cols].astype(F32) + through).astype(BF)
            hop(1, bwd_out, up, c, -1).start()

    @pl.when(section == last)
    def _():
        share_normed()

    token = lax.broadcasted_iota(jnp.int32, (256, RING * TOKENS), 1)
    early = lax.rem(token, TOKENS) < HALF
    for one in n_trades:
        one.wait()
    for half, n_all in enumerate((n_y, n_x)):
        left = jnp.concatenate([n_all[src].reshape(256, TOKENS) for src in range(RING)], axis=1)
        zero = jnp.zeros_like(left)
        lefts[half, 0] = jnp.where(early, left, zero)
        lefts[half, 1] = jnp.where(early, zero, left)
    weights.drain()
    for one in k_trades:
        one.wait()
    for half, k_all, buf in ((0, k_y, x_buf), (1, k_x, y_buf)):
        right = k_all[...].reshape(RING * TOKENS, KVW)
        for step in range(2):
            part = mm(lefts[half, step], right).astype(BF).reshape(2, RING, 32, KVW)
            for there in range(RING):
                buf[there, :, :, step * KVW : (step + 1) * KVW] = part[:, there]
        one = (
            trade(4, "x", lambda there: x_buf.at[there], x_all)
            if buf is x_buf
            else trade(5, "y", lambda there: y_buf.at[there], y_all)
        )
        one.start()
    x_all[place.x] = x_buf[place.x]
    y_all[place.y] = y_buf[place.y]
    trade(4, "x", lambda there: x_buf.at[there], x_all).wait()
    trade(5, "y", lambda there: y_buf.at[there], y_all).wait()
    for start, parts in ((0, x_all), (2, y_all)):
        total = parts[0].astype(F32)
        for src in range(1, RING):
            total = total + parts[src].astype(F32)
        z_buf[start : start + 2] = total.astype(BF)
    z_trade = trade(6, "z", lambda there: z_buf.at[there], z_all)
    z_all[place.z] = z_buf[place.z]
    z_trade.start()
    z_trade.wait()
    grads = z_all[0].astype(F32)
    for src in range(1, RING):
        grads = grads + z_all[src].astype(F32)
    grads = grads * (1.0 / REPLICAS)
    outputs = Gather(
        place,
        [
            (stash_out, 0, 384, "z", "x", "y"),
            (next_out, 0, 384, "z", "y", "x"),
            (stash_out, 384, 128, "x", "y", "z"),
            (next_out, 384, 128, "y", "x", "z"),
        ],
        o_send,
        o_recv,
        (0, 1, 2, 3),
        True,
        (2,),
    )
    own = pl.ds(pl.multiple_of(place.me * 32, 32), 32)
    rows = kv_now[0, own, :]
    first, second = adam_m[0], adam_v[0]
    for step, target in ((0, stash_out), (1, next_out)):
        grad = grads[:, step * KVW : (step + 1) * KVW]
        first_new = beta_first * first.astype(F32) + (1.0 - beta_first) * grad
        second_new = beta_second * second.astype(F32) + (1.0 - beta_second) * grad * grad
        moved = rows.astype(F32) - learn_rate * first_new / (jnp.sqrt(second_new) + adam_eps)
        rows, first, second = moved.astype(BF), first_new.astype(BF), second_new.astype(BF)
        target[place.z, place.y, place.x] = rows
        outputs.begin((step, step + 2))
    m_out[0] = first
    v_out[0] = second
    outputs.finish(range(4))

    outputs.drain()
    drain_hops()


def place_results(*refs):
    sem = refs[12]
    loads, stores = [], []
    for i in range(4):
        for part in range(RING if i < 2 else 1):
            slot = len(loads)
            src, dst, held = (refs[j + i].at[part] for j in (0, 4, 8))
            loads.append(pltpu.make_async_copy(src, held, sem.at[0, slot]))
            stores.append(pltpu.make_async_copy(held, dst, sem.at[1, slot]))
    for load in loads:
        load.start()
    for load, store in zip(loads, stores):
        load.wait()
        store.start()
    for store in stores:
        store.wait()


def body(
    embeddings, cotangent, plan, doc_ids, norm_gain, w_query, w_out, kv_stash, kv_now, adam_m, adam_v
):
    vmem = pl.BlockSpec(memory_space=pltpu.VMEM)
    smem = pl.BlockSpec(memory_space=pltpu.SMEM)
    hbm = pl.BlockSpec(memory_space=pl.ANY)
    dma = pltpu.SemaphoreType.DMA
    version = jax.ShapeDtypeStruct((RING, RING, RING, 32, KVW), BF)
    moment = jax.ShapeDtypeStruct((1, 32, KVW), BF)
    results = pl.pallas_call(
        kernel,
        out_shape=(version, version, moment, moment),
        in_specs=[hbm, hbm, smem, vmem, vmem, vmem, vmem, hbm, hbm, vmem, vmem],
        out_specs=(vmem,) * 4,
        scratch_shapes=[
            pltpu.VMEM((1, 4, 32, WIDTH), BF),
            pltpu.VMEM((1, 4, 32, WIDTH), BF),
            pltpu.VMEM((1, WIDTH, KVW), BF),
            pltpu.VMEM((1, WIDTH, KVW), BF),
            pltpu.VMEM((8, TOKENS), F32),
            pltpu.VMEM((RING, RING, RING, 32, QW), BF),
            pltpu.VMEM((RING, RING, RING, 16, WIDTH), BF),
            pltpu.VMEM((QW, WIDTH), BF),
            pltpu.VMEM((WIDTH, QW), BF),
            pltpu.VMEM((KVW, WIDTH), BF),
            pltpu.VMEM((KVW, WIDTH), BF),
            pltpu.VMEM((TOKENS, WIDTH), BF),
            pltpu.VMEM((TOKENS, WIDTH), BF),
            pltpu.VMEM((TOKENS, WIDTH), BF),
            pltpu.VMEM((TOKENS, WIDTH), BF),
            pltpu.VMEM((TOKENS, WIDTH), F32),
            pltpu.VMEM((TOKENS, 128), F32),
            pltpu.VMEM((TOKENS, QW), BF),
            pltpu.VMEM((TOKENS, KVW), BF),
            pltpu.VMEM((4, TOKENS, 4 * TOKENS), F32),
            pltpu.VMEM((TOKENS, QW), BF),
            pltpu.VMEM((TOKENS, QW), BF),
            pltpu.VMEM((TOKENS, QW), BF),
            pltpu.VMEM((TOKENS, KVW), BF),
            pltpu.VMEM((RING, RING, RING, 32, TOKENS), BF),
            pltpu.VMEM((RING, 2, RING, 32, TOKENS), BF),
            pltpu.VMEM((RING, 2, RING, 32, TOKENS), BF),
            pltpu.VMEM((RING, TOKENS, KVW), BF),
            pltpu.VMEM((RING, TOKENS, KVW), BF),
            pltpu.VMEM((2, 2, 256, RING * TOKENS), BF),
            pltpu.VMEM((RING, 2, 32, 2 * KVW), BF),
            pltpu.VMEM((RING, 2, 32, 2 * KVW), BF),
            pltpu.VMEM((RING, 2, 32, 2 * KVW), BF),
            pltpu.VMEM((RING, 2, 32, 2 * KVW), BF),
            pltpu.VMEM((RING, 32, 2 * KVW), BF),
            pltpu.VMEM((RING, 32, 2 * KVW), BF),
            dma((6, 3)),
            dma((6, 31)),
            dma((4, 3)),
            dma((4, 31)),
            dma((2, CHUNKS)),
            dma((2, CHUNKS)),
            dma((7, RING - 1)),
            dma((7, RING - 1)),
            dma((4,)),
        ],
        compiler_params=pltpu.CompilerParams(
            collective_id=0, has_side_effects=True, vmem_limit_bytes=56 * 1024 * 1024
        ),
    )(embeddings, cotangent, plan, doc_ids, norm_gain, w_query, w_out, kv_stash, kv_now, adam_m, adam_v)
    pieces = 2 * RING + 2
    stash, current, first, second = pl.pallas_call(
        place_results,
        out_shape=[jax.ShapeDtypeStruct(r.shape, BF) for r in results],
        in_specs=[hbm] * 4,
        out_specs=[hbm] * 4,
        scratch_shapes=[pltpu.VMEM(r.shape, BF) for r in results] + [dma((2, pieces))],
        compiler_params=pltpu.CompilerParams(vmem_limit_bytes=60 * 1024 * 1024),
    )(*results)
    shape = (1, WIDTH, KVW)
    return stash.reshape(shape), current.reshape(shape), first, second


def solution(mesh):
    placed = (
        P("replica", None, None, None),
        P("replica", None, None, None),
        P("replica", None),
        P("replica", None, None),
        P("section", None),
        P("section", "replica", None),
        P("section", "replica", None),
        P("section", None, None),
        P("section", None, None),
        P("section", "replica", None),
        P("section", "replica", None),
    )
    return jax.shard_map(
        body,
        mesh=mesh,
        in_specs=placed,
        out_specs=(
            P("section", None, None),
            P("section", None, None),
            P("section", "replica", None),
            P("section", "replica", None),
        ),
        check_vma=False,
    )
```

```python
import functools

import jax
import jax.numpy as jnp
from jax import lax
from jax.experimental import pallas as pl
from jax.experimental.pallas import tpu as pltpu
from jax.sharding import PartitionSpec as P

HEAD = 64
RING = 4
REPLICAS = 64
TOKENS = 128
HALF = 64
WIDTH = 2048
QW = 1024
KVW = 512
WIDE = 512
CHUNKS = 4
BF = jnp.bfloat16
F32 = jnp.float32
MESH = pl.DeviceIdType.MESH

beta_first = 0.9
beta_second = 0.999
learn_rate = 0.003
adam_eps = 1e-08
norm_eps = 1e-05

NN = (((1,), (0,)), ((), ()))
NT = (((1,), (1,)), ((), ()))
TN = (((0,), (0,)), ((), ()))


def mm(a, b, dims=NN):
    return lax.dot_general(a, b, dims, preferred_element_type=F32)


def wrap(v):
    return lax.rem(v + RING, RING)


class Place:
    def __init__(self):
        me = lax.axis_index("replica")
        self.me = me
        self.z = me // 16
        self.y = lax.rem(me // 4, RING)
        self.x = lax.rem(me, RING)
        self.line = {}
        for axis, own in (("z", self.z), ("y", self.y), ("x", self.x)):
            self.line[axis] = [own] + [wrap(own + step) for step in range(1, RING)]

    def on(self, axis, step):
        return self.line[axis][step % RING]

    def at(self, axis, step):
        spot = {"z": self.z, "y": self.y, "x": self.x}
        spot[axis] = self.on(axis, step)
        return (spot["z"] * RING + spot["y"]) * RING + spot["x"]


class Gather:
    def __init__(self, place, parts, send, recv, direct, far, over):
        self.place, self.parts, self.send, self.recv = place, parts, send, recv
        self.direct, self.far, self.over = direct, far, over
        self.peer = {
            (axis, step): place.at(axis, step) for axis in ("x", "y", "z") for step in (1, -1, 2)
        }

    def piece(self, k, da, du=0, dv=0, many=None):
        ref, first, columns, a, u, v = self.parts[k]
        spot = {a: self.place.on(a, da), u: self.place.on(u, du), v: self.place.on(v, dv)}
        if many is not None:
            spot[u] = many
        return ref.at[spot["z"], spot["y"], spot["x"], :, pl.ds(first, columns)]

    def copy(self, k, piece, axis, step, slot):
        stage = 0 if slot < 3 else 1 if slot < 15 else 2
        return pltpu.make_async_remote_copy(
            src_ref=piece,
            dst_ref=piece,
            send_sem=self.send.at[k, stage],
            recv_sem=self.recv.at[k, slot],
            device_id={"replica": self.peer[axis, step]},
            device_id_type=MESH,
        )

    def along_a(self, k, start):
        a = self.parts[k][3]
        for step in (1, -1):
            copy = self.copy(k, self.piece(k, 0 if start else -step), a, step, (1 - step) // 2)
            copy.start() if start else copy.wait_recv()

    def past_a(self, k, start):
        a = self.parts[k][3]
        step = 1 if k % 2 else -1
        source = -step
        if self.far:
            step, source = 2, 0
        copy = self.copy(k, self.piece(k, source if start else 2), a, step, 2)
        copy.start() if start else copy.wait_recv()

    def along_u(self, k, dz, start):
        u = self.parts[k][4]
        for step in (1, -1):
            piece = self.piece(k, dz, 0 if start else -step)
            copy = self.copy(k, piece, u, step, 3 + 3 * (dz % RING) + (1 - step) // 2)
            copy.start() if start else copy.wait_recv()

    def past_u(self, k, dz, start):
        u = self.parts[k][4]
        step = 1 if dz % 2 else -1
        source = -step
        if dz % RING in self.direct:
            step, source = 2, 0
        piece = self.piece(k, dz, source if start else 2)
        copy = self.copy(k, piece, u, step, 3 + 3 * (dz % RING) + 2)
        copy.start() if start else copy.wait_recv()

    def along_v(self, k, dz, start):
        v = self.parts[k][5]
        for step in (1, -1):
            piece = self.piece(k, dz, 0, 0 if start else -step, slice(0, RING))
            copy = self.copy(k, piece, v, step, 15 + 4 * (dz % RING) + (1 - step) // 2)
            copy.start() if start else copy.wait_recv()

    def past_v(self, k, dz, start):
        v = self.parts[k][5]
        if dz % RING in self.over:
            piece = self.piece(k, dz, 0, 0 if start else 2, slice(0, RING))
            copy = self.copy(k, piece, v, 2, 17 + 4 * (dz % RING))
            copy.start() if start else copy.wait_recv()
            return
        for step in (1, -1):
            half = slice(0, 2) if step == 1 else slice(2, RING)
            piece = self.piece(k, dz, 0, -step if start else 2, half)
            copy = self.copy(k, piece, v, step, 17 + 4 * (dz % RING) + (1 - step) // 2)
            copy.start() if start else copy.wait_recv()

    def send_u(self, k, dz):
        self.along_u(k, dz, True)
        if dz % RING in self.direct:
            self.past_u(k, dz, True)

    def take_u(self, k, dz):
        self.along_u(k, dz, False)
        if dz % RING not in self.direct:
            self.past_u(k, dz, True)

    def send_v(self, k, dz):
        self.past_u(k, dz, False)
        self.along_v(k, dz, True)
        if dz % RING in self.over:
            self.past_v(k, dz, True)

    def take_v(self, k, dz):
        self.along_v(k, dz, False)
        if dz % RING not in self.over:
            self.past_v(k, dz, True)

    def begin(self, parts):
        for k in parts:
            self.along_a(k, True)
        for k in parts:
            self.send_u(k, 0)
        for k in parts:
            if self.far:
                self.past_a(k, True)

    def finish(self, parts, settle=None):
        def each(step, *planes):
            for dz in planes:
                for k in parts:
                    step(k, dz)

        each(self.take_u, 0)
        each(self.send_v, 0)
        for k in parts:
            self.along_a(k, False)
            if not self.far:
                self.past_a(k, True)
        each(self.send_u, -1, 1)
        if not self.far:
            each(self.take_u, -1, 1)
            each(self.take_v, 0)
        for k in parts:
            self.past_a(k, False)
        each(self.send_u, 2)
        if self.far:
            each(self.take_u, -1, 1)
        each(self.send_v, -1, 1)
        each(self.take_u, 2)
        each(self.send_v, 2)
        if self.far:
            each(self.take_v, 0)
        each(self.take_v, -1, 1, 2)
        for dz in (0, -1, 1, 2):
            for k in parts:
                self.past_v(k, dz, False)
                if settle is not None:
                    settle(k, dz).start()

    def plane(self, k, dz, ref):
        first, columns, a = self.parts[k][1:4]
        spot = [self.place.on(a, dz) if axis == a else slice(0, RING) for axis in "zyx"]
        return ref.at[spot[0], spot[1], spot[2], :, pl.ds(first, columns)]

    def drain(self):
        for k in range(len(self.parts)):
            ref, first, columns = self.parts[k][:3]
            columns = pl.ds(first, columns)
            sent = (
                ref.at[0, 0, 0:3, :, columns],
                ref.at[0, 0:3, :, :, columns],
                ref.at[0:3, :, :, :, columns],
            )
            for piece, slot in zip(sent, (0, 3, 15)):
                self.copy(k, piece, "x", 1, slot).wait_send()


class Exchange:
    def __init__(self, place, axis, out, into, send, recv):
        self.place, self.axis, self.out, self.into = place, axis, out, into
        self.send, self.recv = send, recv
        self.mine = {"x": place.x, "y": place.y, "z": place.z}[axis]

    def copies(self):
        for step in (1, 3, 2):
            there = self.place.on(self.axis, step)
            source = self.out(there)
            yield there, step, pltpu.make_async_remote_copy(
                src_ref=source,
                dst_ref=self.into.at[self.mine],
                send_sem=self.send.at[step - 1],
                recv_sem=self.recv.at[step - 1],
                device_id={"replica": self.place.at(self.axis, step)},
                device_id_type=MESH,
            )

    def start(self):
        for there, step, copy in self.copies():
            copy.start()

    def wait(self):
        for there, step, copy in self.copies():
            copy.wait_recv()
        for there, step, copy in self.copies():
            copy.wait_send()


def lower_lanes(shape):
    return lax.broadcasted_iota(jnp.int32, shape, len(shape) - 1) < HEAD


def both_halves(block, half):
    low = lower_lanes(block.shape)
    wide = block.astype(F32)
    own = jnp.where(low, wide, 0.0) if half == 0 else jnp.where(low, 0.0, wide)
    return (own + pltpu.roll(own, HEAD, 1)).astype(BF)


def head_rows(ref, group):
    blocks = []
    for j in range(4):
        start = (2 * group + j // 2) * 128
        block = ref[:, start : start + 128]
        low = lower_lanes(block.shape)
        zero = jnp.zeros_like(block)
        blocks.append(jnp.where(low, block, zero) if j % 2 == 0 else jnp.where(low, zero, block))
    return jnp.concatenate(blocks, axis=0)


def put_heads(ref, group, rows):
    low = lower_lanes((TOKENS, 128))
    for b in range(2):
        first = rows[2 * b * TOKENS : (2 * b + 1) * TOKENS]
        second = rows[(2 * b + 1) * TOKENS : (2 * b + 2) * TOKENS]
        start = (2 * group + b) * 128
        ref[:, start : start + 128] = jnp.where(low, first, second).astype(BF)


def kernel(
    emb_in,
    cot_in,
    plan,
    docs,
    gain,
    wq_share,
    wo_share,
    stash_in,
    now_in,
    adam_m,
    adam_v,
    stash_out,
    next_out,
    m_out,
    v_out,
    stash_all,
    next_all,
    emb,
    cot,
    kv_stash,
    kv_now,
    tags,
    wq,
    wo,
    wq_t,
    wo_t,
    stash_t,
    now_t,
    hid,
    up,
    fwd_out,
    bwd_out,
    wide,
    scale,
    q,
    kv,
    probs,
    mixed,
    mixed_grad,
    dq,
    kg,
    n_t,
    n_y,
    n_x,
    k_y,
    k_x,
    lefts,
    x_buf,
    x_all,
    y_buf,
    y_all,
    z_buf,
    z_all,
    w_send,
    w_recv,
    o_send,
    o_recv,
    hop_send,
    hop_recv,
    trade_send,
    trade_recv,
    load_sem,
    settle_sem,
):
    place = Place()
    section = lax.axis_index("section")
    last = RING - 1

    loads = [
        pltpu.make_async_copy(src, dst, load_sem.at[i])
        for i, (src, dst) in enumerate(
            ((emb_in, emb), (cot_in, cot), (stash_in, kv_stash), (now_in, kv_now))
        )
    ]
    for load in loads:
        load.start()

    def load_wait():
        for load in loads:
            load.wait()

    barrier = pltpu.get_barrier_semaphore()
    for axis in ("x", "y", "z"):
        for step in (1, 2, 3):
            pl.semaphore_signal(
                barrier, inc=1, device_id={"replica": place.at(axis, step)}, device_id_type=MESH
            )
    for step in (1, -1):
        pl.semaphore_signal(
            barrier, inc=1, device_id={"section": wrap(section + step)}, device_id_type=MESH
        )
    pl.semaphore_wait(barrier, 11)

    def columns(c, size=WIDE):
        return slice(c * size, (c + 1) * size)

    def hop(way, src, dst, c, to):
        return pltpu.make_async_remote_copy(
            src_ref=src.at[:, columns(c)],
            dst_ref=dst.at[:, columns(c)],
            send_sem=hop_send.at[way, c],
            recv_sem=hop_recv.at[way, c],
            device_id={"section": wrap(section + to)},
            device_id_type=MESH,
        )

    def drain_hops():
        @pl.when(section < last)
        def _():
            for c in range(CHUNKS):
                hop(0, fwd_out, hid, c, 1).wait_send()

        @pl.when(section > 0)
        def _():
            for c in range(CHUNKS):
                hop(1, bwd_out, up, c, -1).wait_send()

    def four(block):
        return block[:, :128] + block[:, 128:256] + block[:, 256:384] + block[:, 384:]

    def allowed():
        tag = jnp.broadcast_to(tags[:1, :], (TOKENS, TOKENS))
        row = lax.broadcasted_iota(jnp.int32, (TOKENS, TOKENS), 0)
        col = lax.broadcasted_iota(jnp.int32, (TOKENS, TOKENS), 1)
        return (tag == tag.T) & (row // 32 == col // 32) & (row <= col)

    def project():
        @pl.when(section == 0)
        def _():
            for i in range(RING):
                hid[i * 32 : (i + 1) * 32, :] = emb[0, plan[0, i]]

        for c in range(CHUNKS):
            cols = columns(c)

            @pl.when(section > 0)
            def _():
                hop(0, fwd_out, hid, c, -1).wait_recv()

            own = hid[:, cols].astype(F32)
            gained = (own * gain[:, cols].astype(F32)).astype(BF)
            squares = four(own * own)
            products = (
                mm(gained, wq[c].reshape(WIDE, QW)),
                mm(gained[:HALF], kv_stash[0, cols, :]),
                mm(gained[HALF:], kv_now[0, cols, :]),
            )
            if c == 0:
                wide[:, :QW] = products[0]
                wide[:HALF, QW : QW + KVW] = products[1]
                wide[HALF:, QW : QW + KVW] = products[2]
                scale[...] = squares
            else:
                wide[:, :QW] += products[0]
                wide[:HALF, QW : QW + KVW] += products[1]
                wide[HALF:, QW : QW + KVW] += products[2]
                scale[...] += squares
        mean = jnp.sum(scale[...], axis=-1, keepdims=True) * (1.0 / WIDTH)
        r = lax.rsqrt(mean + norm_eps)
        scale[...] = jnp.broadcast_to(r, (TOKENS, 128))
        q[...] = (wide[:, :QW] * r).astype(BF)
        kv[...] = (wide[:, QW : QW + KVW] * r).astype(BF)

        mask = jnp.concatenate([allowed()] * 4, axis=1)
        for group in range(4):
            start = (group // 2) * 128
            keys = both_halves(kv[:, start : start + 128], group % 2)
            values = both_halves(kv[:, 256 + start : 256 + start + 128], group % 2)
            score = mm(keys, head_rows(q, group), NT)
            weight = jnp.where(mask, jnp.exp(score * (HEAD**-0.5)), 0.0)
            prob = weight / jnp.sum(weight, axis=0, keepdims=True)
            probs[group] = prob

            @pl.when(section < last)
            def _():
                put_heads(mixed, group, mm(prob.astype(BF), values, TN))

    def prepare():
        def turn(i, carry):
            rows = pl.ds(pl.multiple_of(i * WIDE, WIDE), WIDE)
            wq_t[:, rows] = wq[i].reshape(WIDE, QW).T
            stash_t[:, rows] = kv_stash[0, rows, :].T
            now_t[:, rows] = kv_now[0, rows, :].T
            return carry

        def turn_out(i, carry):
            rows = pl.ds(pl.multiple_of(i * 256, 256), 256)
            wo_t[:, rows] = wo[i].reshape(256, WIDTH).T
            return carry

        lax.fori_loop(0, RING, turn_out, 0)
        lax.fori_loop(0, RING, turn, 0)

    def trade(index, axis, out, into):
        return Exchange(place, axis, out, into, trade_send.at[index], trade_recv.at[index])

    n_trades = (
        trade(0, "y", lambda there: n_t.at[0:2, there], n_y),
        trade(1, "x", lambda there: n_t.at[2:4, :, there], n_x),
    )
    k_trades = (trade(2, "y", lambda there: kg, k_y), trade(3, "x", lambda there: kg, k_x))

    def share_normed():
        for block in range(RING * RING):
            cols = columns(block, 128)
            own = hid[:, cols].astype(F32) * scale[...] * gain[:, cols].astype(F32)
            n_t[block // RING, block % RING] = own.astype(BF).T.reshape(RING, 32, TOKENS)
        n_y[place.y] = n_t[0:2, place.y]
        n_x[place.x] = n_t[2:4, :, place.x]
        for one in n_trades:
            one.start()

    def make_mixed_grad(streamed):
        for c in range(CHUNKS):
            if streamed:
                hop(1, bwd_out, up, c, 1).wait_recv()
            part = mm(up[:, columns(c)], wo_t[columns(c), :])
            if c == 0:
                wide[:, :QW] = part
            elif c < CHUNKS - 1:
                wide[:, :QW] += part
            else:
                mixed_grad[...] = (wide[:, :QW] + part).astype(BF)

    weights = Gather(
        place,
        [
            (wq, 0, 384, "z", "x", "y"),
            (wq, 384, 384, "z", "y", "x"),
            (wq, 768, 256, "x", "y", "z"),
            (wo, 0, 896, "z", "x", "y"),
            (wo, 896, 896, "z", "y", "x"),
            (wo, 1792, 256, "y", "x", "z"),
        ],
        w_send,
        w_recv,
        (0,),
        False,
        (),
    )
    wq[place.z, place.y, place.x] = wq_share[0]
    wo[place.z, place.y, place.x] = wo_share[0]

    weights.begin(range(6))
    for i in range(RING):
        tags[:1, i * 32 : (i + 1) * 32] = docs[0, pl.ds(plan[0, i], 1), :].astype(F32)
    weights.finish(range(6))

    load_wait()

    @pl.when(section == last)
    def _():
        prepare()
        for i in range(RING):
            up[i * 32 : (i + 1) * 32, :] = cot[0, plan[0, i]]
        make_mixed_grad(False)

    project()

    @pl.when(section < last)
    def _():
        for c in range(CHUNKS):
            cols = columns(c)
            fwd_out[:, cols] = (hid[:, cols].astype(F32) + mm(mixed[...], wo[:, :, :, :, cols].reshape(QW, WIDE))).astype(BF)
            hop(0, fwd_out, hid, c, 1).start()
        prepare()
        share_normed()
        make_mixed_grad(True)

    low = lower_lanes((TOKENS, 128))
    folded = []
    for group in range(4):
        start = (group // 2) * 128
        keys = both_halves(kv[:, start : start + 128], group % 2)
        values = both_halves(kv[:, 256 + start : 256 + start + 128], group % 2)
        heads = head_rows(q, group)
        heads_grad = head_rows(mixed_grad, group)
        prob = probs[group]
        prob_grad = mm(values, heads_grad, NT)
        inner = jnp.sum(prob_grad * prob, axis=0, keepdims=True)
        score_grad = (prob * (prob_grad - inner) * (HEAD**-0.5)).astype(BF)
        put_heads(dq, group, mm(score_grad, keys, TN))
        dk = mm(score_grad, heads)
        dv = mm(prob.astype(BF), heads_grad)
        folded.append((dk + pltpu.roll(dk, HEAD, 1), dv + pltpu.roll(dv, HEAD, 1)))
        if group % 2 == 1:
            for part in range(2):
                both = jnp.where(low, folded[group - 1][part], folded[group][part]).astype(BF)
                kg[:, part * 256 + start : part * 256 + start + 128] = both

    k_y[place.y] = kg[...]
    k_x[place.x] = kg[...]
    for one in k_trades:
        one.start()

    @pl.when(section > 0)
    def _():
        total = jnp.zeros((TOKENS, 128), F32)
        for c in range(CHUNKS):
            cols = columns(c)
            first = mm(kg[:HALF, :], stash_t[:, cols])
            second = mm(kg[HALF:, :], now_t[:, cols])
            part = mm(dq[...], wq_t[:, cols]) + jnp.concatenate([first, second], axis=0)
            part = part * gain[:, cols].astype(F32)
            wide[:, cols] = part
            total = total + four(part * hid[:, cols].astype(F32))
        r = scale[...]
        inner = jnp.sum(total, axis=-1, keepdims=True) * (1.0 / WIDTH)
        inner = jnp.broadcast_to(inner, (TOKENS, 128)) * (r * r * r)
        for c in range(CHUNKS):
            for d in range(RING):
                cols = columns(c * RING + d, 128)
                through = wide[:, cols] * r - hid[:, cols].astype(F32) * inner
                bwd_out[:, cols] = (up[:, cols].astype(F32) + through).astype(BF)
            hop(1, bwd_out, up, c, -1).start()

    @pl.when(section == last)
    def _():
        share_normed()

    token = lax.broadcasted_iota(jnp.int32, (256, RING * TOKENS), 1)
    early = lax.rem(token, TOKENS) < HALF
    for one in n_trades:
        one.wait()
    for half, n_all in enumerate((n_y, n_x)):
        left = jnp.concatenate([n_all[src].reshape(256, TOKENS) for src in range(RING)], axis=1)
        zero = jnp.zeros_like(left)
        lefts[half, 0] = jnp.where(early, left, zero)
        lefts[half, 1] = jnp.where(early, zero, left)
    weights.drain()
    for one in k_trades:
        one.wait()
    for half, k_all, buf in ((0, k_y, x_buf), (1, k_x, y_buf)):
        right = k_all[...].reshape(RING * TOKENS, KVW)
        for step in range(2):
            part = mm(lefts[half, step], right).astype(BF).reshape(2, RING, 32, KVW)
            for there in range(RING):
                buf[there, :, :, step * KVW : (step + 1) * KVW] = part[:, there]
        one = (
            trade(4, "x", lambda there: x_buf.at[there], x_all)
            if buf is x_buf
            else trade(5, "y", lambda there: y_buf.at[there], y_all)
        )
        one.start()
    x_all[place.x] = x_buf[place.x]
    y_all[place.y] = y_buf[place.y]
    trade(4, "x", lambda there: x_buf.at[there], x_all).wait()
    trade(5, "y", lambda there: y_buf.at[there], y_all).wait()
    for start, parts in ((0, x_all), (2, y_all)):
        total = parts[0].astype(F32)
        for src in range(1, RING):
            total = total + parts[src].astype(F32)
        z_buf[start : start + 2] = total.astype(BF)
    z_trade = trade(6, "z", lambda there: z_buf.at[there], z_all)
    z_all[place.z] = z_buf[place.z]
    z_trade.start()
    z_trade.wait()
    grads = z_all[0].astype(F32)
    for src in range(1, RING):
        grads = grads + z_all[src].astype(F32)
    grads = grads * (1.0 / REPLICAS)
    outputs = Gather(
        place,
        [
            (stash_all, 0, 384, "z", "x", "y"),
            (next_all, 0, 384, "z", "y", "x"),
            (stash_all, 384, 128, "x", "y", "z"),
            (next_all, 384, 128, "y", "x", "z"),
        ],
        o_send,
        o_recv,
        (0, 1, 2, 3),
        True,
        (2,),
    )
    own = pl.ds(pl.multiple_of(place.me * 32, 32), 32)
    rows = kv_now[0, own, :]
    first, second = adam_m[0], adam_v[0]
    for step, target in ((0, stash_all), (1, next_all)):
        grad = grads[:, step * KVW : (step + 1) * KVW]
        first_new = beta_first * first.astype(F32) + (1.0 - beta_first) * grad
        second_new = beta_second * second.astype(F32) + (1.0 - beta_second) * grad * grad
        moved = rows.astype(F32) - learn_rate * first_new / (jnp.sqrt(second_new) + adam_eps)
        rows, first, second = moved.astype(BF), first_new.astype(BF), second_new.astype(BF)
        target[place.z, place.y, place.x] = rows
        outputs.begin((step, step + 2))
    m_out[0] = first
    v_out[0] = second
    def settle(k, dz):
        full, out = ((stash_all, stash_out), (next_all, next_out))[k % 2]
        return pltpu.make_async_copy(
            outputs.plane(k, dz, full), outputs.plane(k, dz, out), settle_sem.at[k, dz % RING]
        )

    outputs.finish(range(4), settle)
    for dz in (0, -1, 1, 2):
        for k in range(4):
            settle(k, dz).wait()

    outputs.drain()
    drain_hops()


def place_results(*refs):
    sem = refs[12]
    loads, stores = [], []
    for i in range(4):
        for part in range(RING if i < 2 else 1):
            slot = len(loads)
            src, dst, held = (refs[j + i].at[part] for j in (0, 4, 8))
            loads.append(pltpu.make_async_copy(src, held, sem.at[0, slot]))
            stores.append(pltpu.make_async_copy(held, dst, sem.at[1, slot]))
    for load in loads:
        load.start()
    for load, store in zip(loads, stores):
        load.wait()
        store.start()
    for store in stores:
        store.wait()


def body(
    embeddings, cotangent, plan, doc_ids, norm_gain, w_query, w_out, kv_stash, kv_now, adam_m, adam_v
):
    vmem = pl.BlockSpec(memory_space=pltpu.VMEM)
    smem = pl.BlockSpec(memory_space=pltpu.SMEM)
    hbm = pl.BlockSpec(memory_space=pl.ANY)
    dma = pltpu.SemaphoreType.DMA
    version = jax.ShapeDtypeStruct((RING, RING, RING, 32, KVW), BF)
    moment = jax.ShapeDtypeStruct((1, 32, KVW), BF)
    results = pl.pallas_call(
        kernel,
        out_shape=(version, version, moment, moment),
        in_specs=[hbm, hbm, smem, vmem, vmem, vmem, vmem, hbm, hbm, vmem, vmem],
        out_specs=(hbm, hbm, vmem, vmem),
        scratch_shapes=[
            pltpu.VMEM((RING, RING, RING, 32, KVW), BF),
            pltpu.VMEM((RING, RING, RING, 32, KVW), BF),
            pltpu.VMEM((1, 4, 32, WIDTH), BF),
            pltpu.VMEM((1, 4, 32, WIDTH), BF),
            pltpu.VMEM((1, WIDTH, KVW), BF),
            pltpu.VMEM((1, WIDTH, KVW), BF),
            pltpu.VMEM((8, TOKENS), F32),
            pltpu.VMEM((RING, RING, RING, 32, QW), BF),
            pltpu.VMEM((RING, RING, RING, 16, WIDTH), BF),
            pltpu.VMEM((QW, WIDTH), BF),
            pltpu.VMEM((WIDTH, QW), BF),
            pltpu.VMEM((KVW, WIDTH), BF),
            pltpu.VMEM((KVW, WIDTH), BF),
            pltpu.VMEM((TOKENS, WIDTH), BF),
            pltpu.VMEM((TOKENS, WIDTH), BF),
            pltpu.VMEM((TOKENS, WIDTH), BF),
            pltpu.VMEM((TOKENS, WIDTH), BF),
            pltpu.VMEM((TOKENS, WIDTH), F32),
            pltpu.VMEM((TOKENS, 128), F32),
            pltpu.VMEM((TOKENS, QW), BF),
            pltpu.VMEM((TOKENS, KVW), BF),
            pltpu.VMEM((4, TOKENS, 4 * TOKENS), F32),
            pltpu.VMEM((TOKENS, QW), BF),
            pltpu.VMEM((TOKENS, QW), BF),
            pltpu.VMEM((TOKENS, QW), BF),
            pltpu.VMEM((TOKENS, KVW), BF),
            pltpu.VMEM((RING, RING, RING, 32, TOKENS), BF),
            pltpu.VMEM((RING, 2, RING, 32, TOKENS), BF),
            pltpu.VMEM((RING, 2, RING, 32, TOKENS), BF),
            pltpu.VMEM((RING, TOKENS, KVW), BF),
            pltpu.VMEM((RING, TOKENS, KVW), BF),
            pltpu.VMEM((2, 2, 256, RING * TOKENS), BF),
            pltpu.VMEM((RING, 2, 32, 2 * KVW), BF),
            pltpu.VMEM((RING, 2, 32, 2 * KVW), BF),
            pltpu.VMEM((RING, 2, 32, 2 * KVW), BF),
            pltpu.VMEM((RING, 2, 32, 2 * KVW), BF),
            pltpu.VMEM((RING, 32, 2 * KVW), BF),
            pltpu.VMEM((RING, 32, 2 * KVW), BF),
            dma((6, 3)),
            dma((6, 31)),
            dma((4, 3)),
            dma((4, 31)),
            dma((2, CHUNKS)),
            dma((2, CHUNKS)),
            dma((7, RING - 1)),
            dma((7, RING - 1)),
            dma((4,)),
            dma((4, RING)),
        ],
        compiler_params=pltpu.CompilerParams(
            collective_id=0, has_side_effects=True, vmem_limit_bytes=56 * 1024 * 1024
        ),
    )(embeddings, cotangent, plan, doc_ids, norm_gain, w_query, w_out, kv_stash, kv_now, adam_m, adam_v)
    pieces = 2 * RING + 2
    stash, current, first, second = pl.pallas_call(
        place_results,
        out_shape=[jax.ShapeDtypeStruct(r.shape, BF) for r in results],
        in_specs=[hbm] * 4,
        out_specs=[hbm] * 4,
        scratch_shapes=[pltpu.VMEM(r.shape, BF) for r in results] + [dma((2, pieces))],
        compiler_params=pltpu.CompilerParams(vmem_limit_bytes=60 * 1024 * 1024),
    )(*results)
    shape = (1, WIDTH, KVW)
    return stash.reshape(shape), current.reshape(shape), first, second


def solution(mesh):
    placed = (
        P("replica", None, None, None),
        P("replica", None, None, None),
        P("replica", None),
        P("replica", None, None),
        P("section", None),
        P("section", "replica", None),
        P("section", "replica", None),
        P("section", None, None),
        P("section", None, None),
        P("section", "replica", None),
        P("section", "replica", None),
    )
    return jax.shard_map(
        body,
        mesh=mesh,
        in_specs=placed,
        out_specs=(
            P("section", None, None),
            P("section", None, None),
            P("section", "replica", None),
            P("section", "replica", None),
        ),
        check_vma=False,
    )
```
